512 devices in a mesh: sub: 8 (over z), row: 4 (over x_lo, core), col: 16 (over y, x_hi).
Axes of the slice: x: 4 (x_hi: 2, x_lo: 2; x = x_hi * 2 + x_lo), y: 8, z: 8, core: 2. Of those that a mesh axis runs over, the one named last changes fastest.
Arguments:
- parent_front: float32 [16, 16, 32, 8192], P(None, 'col', None, ('sub', 'row')), as said below
- child_schur: float32 [8192, 4096], P(('sub', 'row', 'col')), as said below
- index_map: int32 [2, 256], replicated, may hold values from 0 to 511, as said below
Outputs:
- factored_front: float32 [16, 16, 32, 8192], P(None, 'col', None, ('sub', 'row'))
The draws below stay inside these ranges and needn't reach their ends.
Inputs may be any that keep to these rules, and one draw needn't show every extreme that they name: parent_front is symmetric, and the front assembled with both children is positive definite. `child_schur`: each child's block is symmetric. index_map[c] holds distinct blocks for each c; with g = c * 256 + j and h = (g // 1) % 16, block f = index_map[c, j] satisfies (f * 16 // 32) % 16 == h; every front block receives a block of at least one child.
All inputs are finite; a program needn't handle non-finite values.
Results may differ from the reference program's by a relative error of at most 0.0001.
Values sent between devices are 32-bit elements; how exact they have to be, the bound alone decides.
No kernel may reach another device: no remote copies, remote signals or barrier semaphores. Data moves between devices by JAX's collectives and lax.ppermute only.
A program may use at most 64 MiB of HBM per device.

```python
import math
import jax
import jax.numpy as jnp
from jax import lax

F = 8192
C = 4096
PW = 512
PANELS = 2
BLK = 16
CA = 16
NBC = 32
DR = 16
NE = 1024
N_COL = 16


def draw_parent_front(key, part):
    key = jax.random.fold_in(key, 11)
    noise_key, diag_key = jax.random.split(key, 2)
    noise = jax.random.normal(noise_key, (F, F), jnp.float32)
    sym = (noise + noise.T) * (1.75 / math.sqrt(2.0 * F))
    diag_vals = 5.5 * jnp.exp(jax.random.uniform(diag_key, (F,), jnp.float32, 0.0, math.log(2.0)))
    front = sym + jnp.diag(diag_vals)
    return front.reshape(CA, N_COL, NBC, F)


def draw_child_schur(key, part):
    key = jax.random.fold_in(key, 17)
    noise = jax.random.normal(key, (2, C, C), jnp.float32)
    sym = (noise + noise.transpose(0, 2, 1)) * (1.75 / math.sqrt(2.0 * C))
    return sym.reshape(2 * C, C)


def draw_index_map(key, part):
    key = jax.random.fold_in(key, 29)
    child_blocks = C // BLK
    per_device = DR // BLK
    slots = F // BLK // N_COL
    used = child_blocks // N_COL
    stride = NBC // BLK
    keys = jax.random.split(key, N_COL)
    orders = jax.vmap(lambda single: jax.random.permutation(single, slots))(keys)
    within = jnp.arange(child_blocks)
    results = []
    for child_id in range(2):
        stacked = child_id * child_blocks + within
        device = stacked // per_device
        owner = device % N_COL
        column_rank = device // N_COL - child_id * (child_blocks // per_device) // N_COL
        position = column_rank * per_device + stacked % per_device
        position = position + child_id * (slots - used)
        chosen = orders[owner, position]
        target = (chosen // stride * N_COL + owner) * stride + chosen % stride
        results.append(target)
    return jnp.stack(results).astype(jnp.int32)


def setup_inputs(seed: int = 0) -> dict:
    key_of = jax.random.split(jax.random.key(seed), 4)
    parent_front = draw_parent_front(jax.random.fold_in(key_of[3], 71), 0)
    child_schur = draw_child_schur(jax.random.fold_in(key_of[3], 71), 0)
    index_map = draw_index_map(jax.random.fold_in(key_of[3], 71), 0)
    return dict(parent_front=parent_front, child_schur=child_schur, index_map=index_map)


highest = lax.Precision.HIGHEST

def reference(parent_front, child_schur, index_map):
    front = parent_front.reshape(F, F)
    child_blocks = C // BLK
    front_blocks = F // BLK
    for child_id in range(2):
        part = child_schur[child_id * C:(child_id + 1) * C]
        part = part.reshape(child_blocks, BLK, child_blocks, BLK).transpose(0, 2, 1, 3)
        targets = index_map[child_id]
        shaped = front.reshape(front_blocks, BLK, front_blocks, BLK)
        shaped = shaped.at[targets[:, None], :, targets[None, :], :].add(part)
        front = shaped.reshape(F, F)
    factored = jnp.zeros((F, F), jnp.float32)
    columns = jnp.arange(F)
    for number in range(PANELS):
        begin_col = number * PW
        end_col = begin_col + PW
        factor = jnp.linalg.cholesky(front[begin_col:end_col, begin_col:end_col])
        solved = lax.linalg.triangular_solve(factor, front[begin_col:end_col, :], left_side=True, lower=True)
        solved = jnp.where(columns[None, :] >= begin_col, solved, jnp.float32(0.0))
        factored = factored.at[begin_col:end_col, :].set(solved)
        trailing = solved[:, end_col:]
        update = jnp.dot(trailing.T.astype(jnp.float32), trailing.astype(jnp.float32), precision=highest, preferred_element_type=jnp.float32)
        front = front.at[end_col:, end_col:].add(-update)
    factored = factored.at[NE:, NE:].set(front[NE:, NE:])
    return factored.reshape(CA, N_COL, NBC, F)
```

```python
import functools

import jax
import jax.numpy as jnp
from jax import lax
from jax.experimental import pallas as pl
from jax.experimental.pallas import tpu as pltpu
from jax.sharding import PartitionSpec as P

BLK = 16
TILE = 128
STEP = 8
SUBS = 8
ROWS = 4
COLS = 16
SHARDS = SUBS * ROWS
WIDE = 256
PANEL = 512
HIGHEST = lax.Precision.HIGHEST

VMEM = pl.BlockSpec(memory_space=pltpu.VMEM)
SMEM = pl.BlockSpec(memory_space=pltpu.SMEM)
PARAMS = pltpu.CompilerParams(vmem_limit_bytes=40 << 20)


def contract(a, b, dims):
    return lax.dot_general(
        a, b, ((dims[:1], dims[1:]), ((), ())), precision=HIGHEST, preferred_element_type=jnp.float32
    )


def dot(a, b):
    return contract(a, b, (1, 0))


def dot_t(a, b):
    return contract(a, b, (1, 1))


def t_dot(a, b):
    return contract(a, b, (0, 0))


def spread_kernel(where_ref, map_ref, child_ref, out_ref):
    child = where_ref[0]
    out_ref[...] = jnp.zeros_like(out_ref)
    lane_block = lax.broadcasted_iota(jnp.int32, (BLK, TILE), 1) // BLK

    def body(tile, carry):
        rows = child_ref[:, pl.ds(pl.multiple_of(tile * TILE, TILE), TILE)]
        for part in range(TILE // BLK):
            block = map_ref[child, tile * (TILE // BLK) + part]
            place = block % (TILE // BLK)
            target = block // (TILE // BLK)
            shift = (place - part + TILE // BLK) % (TILE // BLK) * BLK
            moved = pltpu.roll(rows, shift, 1)
            out_ref[target] = jnp.where(lane_block == place, moved, out_ref[target])
        return carry

    lax.fori_loop(0, child_ref.shape[1] // TILE, body, 0)


def spread_rows(where, index_map, child):
    return pl.pallas_call(
        spread_kernel,
        out_shape=jax.ShapeDtypeStruct((2 * SHARDS, BLK, TILE), jnp.float32),
        in_specs=[SMEM, SMEM, VMEM],
        out_specs=VMEM,
        compiler_params=PARAMS,
        name="spread_rows",
    )(where, index_map, child)


def place_kernel(where_ref, map_ref, received_ref, parent_ref, out_ref):
    col = where_ref[1]

    def body(source, carry):
        child = source // (SHARDS // 2)
        block = map_ref[child, source % (SHARDS // 2) * COLS + col]
        slot = block // (2 * COLS) * 2 + block % 2
        for half in range(2):
            lanes = slice(half * TILE, (half + 1) * TILE)
            out_ref[slot, :, lanes] = parent_ref[slot, :, lanes] + received_ref[source, half]
        return carry

    lax.fori_loop(0, SHARDS, body, 0)


def place(where, index_map, received, parent):
    return pl.pallas_call(
        place_kernel,
        out_shape=jax.ShapeDtypeStruct((SHARDS, BLK, WIDE), jnp.float32),
        in_specs=[SMEM, SMEM, VMEM, VMEM],
        out_specs=VMEM,
        compiler_params=PARAMS,
        name="place",
    )(where, index_map, received, parent)


def tree_sum(terms):
    while len(terms) > 1:
        terms = [sum(terms[i : i + 2]) for i in range(0, len(terms), 2)]
    return terms[0]


def factor_tile(read, out_ref):
    full = (8, TILE)
    groups = TILE // 8
    sub = lax.broadcasted_iota(jnp.int32, full, 0)
    lane = lax.broadcasted_iota(jnp.int32, full, 1)
    a = [read(h) for h in range(groups)]
    e = [jnp.where(lane == sub + 8 * h, jnp.float32(1), jnp.float32(0)) for h in range(groups)]
    for j in range(0, TILE, STEP):
        g, r = divmod(j, 8)
        col = [
            [jnp.broadcast_to(a[h][:, j + t : j + t + 1], full) for t in range(STEP)]
            for h in range(g, groups)
        ]
        p = [
            [jnp.broadcast_to(col[0][t][r + s : r + s + 1, :], full) for t in range(s + 1)]
            for s in range(STEP)
        ]
        ua = [jnp.broadcast_to(a[g][r + s : r + s + 1, :], full) for s in range(STEP)]
        ue = [jnp.broadcast_to(e[g][r + s : r + s + 1, :], full) for s in range(STEP)]
        rd = [None] * STEP
        low = [[None] * STEP for _ in range(STEP)]
        for t in range(STEP):
            rd[t] = 1.0 / p[t][t]
            for s in range(t + 1, STEP):
                low[s][t] = p[s][t] * rd[t]
            for s in range(t + 1, STEP):
                for q in range(t + 1, s + 1):
                    p[s][q] = p[s][q] - low[s][t] * p[q][t]
            for s in range(t + 1, STEP):
                ua[s] = ua[s] - low[s][t] * ua[t]
                ue[s] = ue[s] - low[s][t] * ue[t]
        for s in range(STEP):
            out_ref[j + s : j + s + 1, :] = (ue[s] * lax.rsqrt(p[s][s]))[0:1, :]
        if j + STEP >= TILE:
            break
        za = [ua[s] * rd[s] for s in range(STEP)]
        ze = [ue[s] * rd[s] for s in range(STEP)]
        for t in range(STEP - 1, 0, -1):
            for s in range(t):
                za[s] = za[s] - low[t][s] * za[t]
                ze[s] = ze[s] - low[t][s] * ze[t]
        for h in range(g, groups):
            if h == g and r + STEP >= 8:
                continue
            c = col[h - g]
            da = tree_sum([c[t] * za[t] for t in range(STEP)])
            de = tree_sum([c[t] * ze[t] for t in range(STEP)])
            if h == g:
                da = jnp.where(sub >= r + STEP, da, 0.0)
                de = jnp.where(sub >= r + STEP, de, 0.0)
            a[h] = a[h] - da
            e[h] = e[h] - de


def invert_factor(m_ref, w_ref, t_ref):
    tiles = m_ref.shape[0] // TILE
    w_ref[...] = jnp.zeros_like(w_ref)

    def body(b, carry):
        low = pl.multiple_of(b * TILE, TILE)
        factor_tile(
            lambda h: m_ref[pl.ds(pl.multiple_of(low + 8 * h, 8), 8), pl.ds(low, TILE)], t_ref
        )
        for c in range(tiles):

            @pl.when(b == c)
            def _():
                lo, hi = c * TILE, (c + 1) * TILE
                t = t_ref[...]
                if c:
                    w_ref[lo:hi, :lo] = dot(t, w_ref[lo:hi, :lo])
                w_ref[lo:hi, lo:hi] = t
                if c + 1 < tiles:
                    x = dot(t, m_ref[lo:hi, hi:])
                    m_ref[hi:, hi:] = m_ref[hi:, hi:] - t_dot(x, x)
                    w_ref[hi:, :hi] = w_ref[hi:, :hi] - t_dot(x, w_ref[lo:hi, :hi])

        return carry

    lax.fori_loop(0, tiles, body, 0)


def fill(m_ref, core, own_ref, other_ref):
    own = pl.multiple_of(core * WIDE, WIDE)
    other = pl.multiple_of((1 - core) * WIDE, WIDE)
    for slot in range(SHARDS):
        rows = slice(slot * BLK, (slot + 1) * BLK)
        m_ref[rows, pl.ds(own, WIDE)] = own_ref[slot]
        m_ref[rows, pl.ds(other, WIDE)] = other_ref[slot]


def first_kernel(where_ref, own_ref, other_ref, w_ref, m_ref, t_ref):
    fill(m_ref, where_ref[2] % 2, own_ref, other_ref)
    invert_factor(m_ref, w_ref, t_ref)


def first_factor(where, own, other):
    return pl.pallas_call(
        first_kernel,
        out_shape=jax.ShapeDtypeStruct((PANEL, PANEL), jnp.float32),
        in_specs=[SMEM, VMEM, VMEM],
        out_specs=VMEM,
        scratch_shapes=[
            pltpu.VMEM((PANEL, PANEL), jnp.float32),
            pltpu.VMEM((TILE, TILE), jnp.float32),
        ],
        compiler_params=PARAMS,
        cost_estimate=pl.CostEstimate(flops=60_000_000_000, bytes_accessed=4 << 20, transcendentals=0),
        name="first_factor",
    )(where, own, other)


def second_kernel(where_ref, inv_ref, up_own, up_other, low_own, low_other, w_ref, x_ref, m_ref, t_ref):
    core = where_ref[2] % 2
    fill(m_ref, core, up_own, up_other)
    x_ref[...] = dot(inv_ref[...], m_ref[...])
    fill(m_ref, core, low_own, low_other)
    m_ref[...] = m_ref[...] - t_dot(x_ref[...], x_ref[...])
    invert_factor(m_ref, w_ref, t_ref)


def second_factor(where, inv, up_own, up_other, low_own, low_other):
    shape = jax.ShapeDtypeStruct((PANEL, PANEL), jnp.float32)
    return pl.pallas_call(
        second_kernel,
        out_shape=(shape, shape),
        in_specs=[SMEM] + [VMEM] * 5,
        out_specs=(VMEM, VMEM),
        scratch_shapes=[
            pltpu.VMEM((PANEL, PANEL), jnp.float32),
            pltpu.VMEM((TILE, TILE), jnp.float32),
        ],
        compiler_params=PARAMS,
        cost_estimate=pl.CostEstimate(flops=60_000_000_000, bytes_accessed=8 << 20, transcendentals=0),
        name="second_factor",
    )(where, inv, up_own, up_other, low_own, low_other)


def finish_kernel(
    where_ref, inv0_ref, inv1_ref, x01_ref, cols_ref, row0, row1, row2, row3, front_ref, out_ref,
    rows_ref, cols0_ref, cols1_ref,
):
    col, row, shard = where_ref[1], where_ref[2], where_ref[3]
    for number, ref in enumerate((row0, row1, row2, row3)):
        chunk = (row // 2 ^ number // 2) * 2 + (row % 2 ^ number % 2)
        low = pl.multiple_of(chunk * WIDE, WIDE)
        for slot in range(SHARDS):
            rows_ref[slot * BLK : (slot + 1) * BLK, pl.ds(low, WIDE)] = ref[slot]
    for q in range(COLS):
        for half in range(2):
            at = slice(q * 2 * BLK + half * BLK, q * 2 * BLK + (half + 1) * BLK)
            cols0_ref[at, :] = cols_ref[q, half]
            cols1_ref[at, :] = cols_ref[q, 2 + half]
    r0 = dot_t(rows_ref[:, :PANEL], inv0_ref[...])
    c0 = dot(inv0_ref[...], cols0_ref[...])
    cols0_ref[...] = c0
    r1 = dot_t(rows_ref[:, PANEL:] - dot(r0, x01_ref[...]), inv1_ref[...])
    c1 = dot(inv1_ref[...], cols1_ref[...] - t_dot(x01_ref[...], c0))
    cols1_ref[...] = c1
    update = dot(r0, c0) + dot(r1, c1)
    live = (shard >= ROWS).astype(jnp.float32)
    for slot in range(4, SHARDS):
        rows = slice(slot * BLK, (slot + 1) * BLK)
        out_ref[slot] = (front_ref[slot] - update[rows]) * live
    mine = pl.multiple_of(col * 2 * BLK, 2 * BLK)
    past = (shard >= ROWS // 2).astype(jnp.float32)
    for half in range(2):
        out_ref[half] = cols0_ref[pl.ds(mine + half * BLK, BLK), :]
        out_ref[2 + half] = cols1_ref[pl.ds(mine + half * BLK, BLK), :] * past


def finish(where, inv0, inv1, x01, cols, rows, front):
    return pl.pallas_call(
        finish_kernel,
        out_shape=jax.ShapeDtypeStruct((SHARDS, BLK, WIDE), jnp.float32),
        in_specs=[SMEM] + [VMEM] * 9,
        out_specs=VMEM,
        scratch_shapes=[
            pltpu.VMEM((PANEL, 2 * PANEL), jnp.float32),
            pltpu.VMEM((PANEL, WIDE), jnp.float32),
            pltpu.VMEM((PANEL, WIDE), jnp.float32),
        ],
        compiler_params=PARAMS,
        name="finish",
    )(where, inv0, inv1, x01, cols, *rows, front)


def swap(x, axis, bit):
    return lax.ppermute(x, axis, [(i, i ^ bit) for i in range(ROWS)])


def to_all(x, axis, count):
    return lax.all_to_all(
        jnp.broadcast_to(x[None], (count, *x.shape)), axis, split_axis=0, concat_axis=0, tiled=True
    )


def exchange(x, axis):
    return lax.all_to_all(x, axis, split_axis=0, concat_axis=0, tiled=True)


def local(parent_front, child_schur, index_map):
    sub, row, col = (lax.axis_index(name) for name in ("sub", "row", "col"))
    shard = sub * ROWS + row
    where = jnp.stack([shard // (SHARDS // 2), col, row, shard]).astype(jnp.int32)
    parent = parent_front.reshape(SHARDS, BLK, WIDE)

    chunk = exchange(parent.reshape(SUBS, SHARDS // SUBS, BLK, WIDE), "sub")[0]
    parent_low = to_all(chunk, "sub", SUBS).reshape(SHARDS, BLK, WIDE)

    spread = spread_rows(where, index_map, child_schur).reshape(SHARDS, 2, BLK, TILE)
    low = jnp.broadcast_to(spread[None, :ROWS], (SUBS, ROWS, 2, BLK, TILE))
    low = exchange(low.reshape(SHARDS, 2, BLK, TILE), ("sub", "row"))
    rows = place(where, index_map, low, parent_low)
    pivots = to_all(rows[:4], "col", COLS)

    received = exchange(spread, ("sub", "row"))
    front = place(where, index_map, received, parent)
    cols = to_all(front[:4], "col", COLS)

    upper = pivots[:, :2].reshape(SHARDS, BLK, WIDE)
    lower = pivots[:, 2:].reshape(SHARDS, BLK, WIDE)
    left = row < 2
    crossed = swap(jnp.where(left, upper, lower), "row", 2)
    diag0 = jnp.where(left, upper, crossed)
    diag1 = jnp.where(left, crossed, lower)
    inv0 = first_factor(where, diag0, swap(diag0, "row", 1))
    above = jnp.where(left, swap(upper, "row", 2), upper)
    inv1, x01 = second_factor(
        where, inv0, above, swap(above, "row", 1), diag1, swap(diag1, "row", 1)
    )
    across = swap(rows, "row", 2)
    pieces = (rows, swap(rows, "row", 1), across, swap(across, "row", 1))
    out = finish(where, inv0, inv1, x01, cols, pieces, front)
    return out.reshape(parent_front.shape)


def solution(mesh):
    spec = P(None, "col", None, ("sub", "row"))
    in_specs = (spec, P(("sub", "row", "col"), None), P())
    return jax.shard_map(local, mesh=mesh, in_specs=in_specs, out_specs=spec, check_vma=False)
```

```python
import functools

import jax
import jax.numpy as jnp
from jax import lax
from jax.experimental import pallas as pl
from jax.experimental.pallas import tpu as pltpu
from jax.sharding import PartitionSpec as P

BLK = 16
TILE = 128
STEP = 8
SUBS = 8
ROWS = 4
COLS = 16
SHARDS = SUBS * ROWS
WIDE = 256
PANEL = 512
HIGHEST = lax.Precision.HIGHEST

VMEM = pl.BlockSpec(memory_space=pltpu.VMEM)
SMEM = pl.BlockSpec(memory_space=pltpu.SMEM)


def params(mib):
    return pltpu.CompilerParams(vmem_limit_bytes=mib << 20)


def contract(a, b, dims):
    return lax.dot_general(
        a, b, ((dims[:1], dims[1:]), ((), ())), precision=HIGHEST, preferred_element_type=jnp.float32
    )


def dot(a, b):
    return contract(a, b, (1, 0))


def dot_t(a, b):
    return contract(a, b, (1, 1))


def t_dot(a, b):
    return contract(a, b, (0, 0))


def spread_kernel(where_ref, map_ref, child_ref, out_ref):
    child = where_ref[0]
    out_ref[...] = jnp.zeros_like(out_ref)
    lane_block = lax.broadcasted_iota(jnp.int32, (BLK, TILE), 1) // BLK

    def body(tile, carry):
        rows = child_ref[:, pl.ds(pl.multiple_of(tile * TILE, TILE), TILE)]
        for part in range(TILE // BLK):
            block = map_ref[child, tile * (TILE // BLK) + part]
            place = block % (TILE // BLK)
            target = block // (TILE // BLK)
            shift = (place - part + TILE // BLK) % (TILE // BLK) * BLK
            moved = pltpu.roll(rows, shift, 1)
            out_ref[target] = jnp.where(lane_block == place, moved, out_ref[target])
        return carry

    lax.fori_loop(0, child_ref.shape[1] // TILE, body, 0)


def spread_rows(where, index_map, child):
    return pl.pallas_call(
        spread_kernel,
        out_shape=jax.ShapeDtypeStruct((2 * SHARDS, BLK, TILE), jnp.float32),
        in_specs=[SMEM, SMEM, VMEM],
        out_specs=VMEM,
        compiler_params=params(4),
        name="spread_rows",
    )(where, index_map, child)


def place_kernel(where_ref, map_ref, received_ref, parent_ref, out_ref):
    col = where_ref[1]

    def body(source, carry):
        child = source // (SHARDS // 2)
        block = map_ref[child, source % (SHARDS // 2) * COLS + col]
        slot = block // (2 * COLS) * 2 + block % 2
        for half in range(2):
            lanes = slice(half * TILE, (half + 1) * TILE)
            out_ref[slot, :, lanes] = parent_ref[slot, :, lanes] + received_ref[source, half]
        return carry

    lax.fori_loop(0, SHARDS, body, 0)


def place(where, index_map, received, parent):
    return pl.pallas_call(
        place_kernel,
        out_shape=jax.ShapeDtypeStruct((SHARDS, BLK, WIDE), jnp.float32),
        in_specs=[SMEM, SMEM, VMEM, VMEM],
        out_specs=VMEM,
        compiler_params=params(6),
        name="place",
    )(where, index_map, received, parent)


def corner_kernel(where_ref, map_ref, received_ref, parent_ref, out_ref):
    col = where_ref[1]

    def body(source, carry):
        child = source // (SHARDS // 2)
        block = map_ref[child, source % (SHARDS // 2) * COLS + col]
        slot = block // (2 * COLS) * 2 + block % 2

        @pl.when(slot < 2)
        def _():
            out_ref[slot] = parent_ref[slot] + received_ref[source]

        return carry

    lax.fori_loop(0, SHARDS, body, 0)


def place_corner(where, index_map, received, parent):
    return pl.pallas_call(
        corner_kernel,
        out_shape=jax.ShapeDtypeStruct((2, BLK, TILE), jnp.float32),
        in_specs=[SMEM, SMEM, VMEM, VMEM],
        out_specs=VMEM,
        compiler_params=params(4),
        name="place_corner",
    )(where, index_map, received, parent)


def tree_sum(terms):
    while len(terms) > 1:
        terms = [sum(terms[i : i + 2]) for i in range(0, len(terms), 2)]
    return terms[0]


def factor_tile(read, out_ref):
    full = (8, TILE)
    groups = TILE // 8
    sub = lax.broadcasted_iota(jnp.int32, full, 0)
    lane = lax.broadcasted_iota(jnp.int32, full, 1)
    a = [read(h) for h in range(groups)]
    e = [jnp.where(lane == sub + 8 * h, jnp.float32(1), jnp.float32(0)) for h in range(groups)]
    for j in range(0, TILE, STEP):
        g, r = divmod(j, 8)
        col = [
            [jnp.broadcast_to(a[h][:, j + t : j + t + 1], full) for t in range(STEP)]
            for h in range(g, groups)
        ]
        p = [
            [jnp.broadcast_to(col[0][t][r + s : r + s + 1, :], full) for t in range(s + 1)]
            for s in range(STEP)
        ]
        ua = [jnp.broadcast_to(a[g][r + s : r + s + 1, :], full) for s in range(STEP)]
        ue = [jnp.broadcast_to(e[g][r + s : r + s + 1, :], full) for s in range(STEP)]
        rd = [None] * STEP
        low = [[None] * STEP for _ in range(STEP)]
        for t in range(STEP):
            rd[t] = 1.0 / p[t][t]
            for s in range(t + 1, STEP):
                low[s][t] = p[s][t] * rd[t]
            for s in range(t + 1, STEP):
                for q in range(t + 1, s + 1):
                    p[s][q] = p[s][q] - low[s][t] * p[q][t]
            for s in range(t + 1, STEP):
                ua[s] = ua[s] - low[s][t] * ua[t]
                ue[s] = ue[s] - low[s][t] * ue[t]
        for s in range(STEP):
            out_ref[j + s : j + s + 1, :] = (ue[s] * lax.rsqrt(p[s][s]))[0:1, :]
        if j + STEP >= TILE:
            break
        za = [ua[s] * rd[s] for s in range(STEP)]
        ze = [ue[s] * rd[s] for s in range(STEP)]
        for t in range(STEP - 1, 0, -1):
            for s in range(t):
                za[s] = za[s] - low[t][s] * za[t]
                ze[s] = ze[s] - low[t][s] * ze[t]
        for h in range(g, groups):
            if h == g and r + STEP >= 8:
                continue
            c = col[h - g]
            da = tree_sum([c[t] * za[t] for t in range(STEP)])
            de = tree_sum([c[t] * ze[t] for t in range(STEP)])
            if h == g:
                da = jnp.where(sub >= r + STEP, da, 0.0)
                de = jnp.where(sub >= r + STEP, de, 0.0)
            a[h] = a[h] - da
            e[h] = e[h] - de


def invert_factor(m_ref, w_ref, t_ref):
    tiles = m_ref.shape[0] // TILE
    w_ref[...] = jnp.zeros_like(w_ref)

    def body(b, carry):
        low = pl.multiple_of(b * TILE, TILE)
        factor_tile(
            lambda h: m_ref[pl.ds(pl.multiple_of(low + 8 * h, 8), 8), pl.ds(low, TILE)], t_ref
        )
        for c in range(tiles):

            @pl.when(b == c)
            def _():
                lo, hi = c * TILE, (c + 1) * TILE
                t = t_ref[...]
                if c:
                    w_ref[lo:hi, :lo] = dot(t, w_ref[lo:hi, :lo])
                w_ref[lo:hi, lo:hi] = t
                if c + 1 < tiles:
                    x = dot(t, m_ref[lo:hi, hi:])
                    m_ref[hi:, hi:] = m_ref[hi:, hi:] - t_dot(x, x)
                    w_ref[hi:, :hi] = w_ref[hi:, :hi] - t_dot(x, w_ref[lo:hi, :hi])

        return carry

    lax.fori_loop(0, tiles, body, 0)


def corner_tile(row):
    return row % 2 * 2 + row // 2


def first_kernel(corner_ref, w_ref, m_ref, t_ref):
    for row in range(ROWS):
        low = corner_tile(row) * TILE
        m_ref[:, low : low + TILE] = corner_ref[row]
    invert_factor(m_ref, w_ref, t_ref)


def first_factor(corner):
    return pl.pallas_call(
        first_kernel,
        out_shape=jax.ShapeDtypeStruct((PANEL, PANEL), jnp.float32),
        in_specs=[VMEM],
        out_specs=VMEM,
        scratch_shapes=[
            pltpu.VMEM((PANEL, PANEL), jnp.float32),
            pltpu.VMEM((TILE, TILE), jnp.float32),
        ],
        compiler_params=params(8),
        cost_estimate=pl.CostEstimate(flops=60_000_000_000, bytes_accessed=4 << 20, transcendentals=0),
        name="first_factor",
    )(corner)


def fill(row, refs, into):
    for number, ref in enumerate(refs):
        chunk = (row // 2 ^ number // 2) * 2 + (row % 2 ^ number % 2)
        low = pl.multiple_of(chunk * WIDE, WIDE)
        for slot in range(SHARDS):
            into[slot * BLK : (slot + 1) * BLK, pl.ds(low, WIDE)] = ref[slot]


def second_kernel(where_ref, inv_ref, own, core, across, both, w_ref, x_ref, a_ref, m_ref, t_ref):
    fill(where_ref[2], (own, core, across, both), a_ref)
    x_ref[...] = dot_t(inv_ref[...], a_ref[:, :PANEL])
    m_ref[...] = a_ref[:, PANEL:] - t_dot(x_ref[...], x_ref[...])
    invert_factor(m_ref, w_ref, t_ref)


def second_factor(where, inv, pieces):
    shape = jax.ShapeDtypeStruct((PANEL, PANEL), jnp.float32)
    return pl.pallas_call(
        second_kernel,
        out_shape=(shape, shape),
        in_specs=[SMEM] + [VMEM] * 5,
        out_specs=(VMEM, VMEM),
        scratch_shapes=[
            pltpu.VMEM((PANEL, 2 * PANEL), jnp.float32),
            pltpu.VMEM((PANEL, PANEL), jnp.float32),
            pltpu.VMEM((TILE, TILE), jnp.float32),
        ],
        compiler_params=params(16),
        cost_estimate=pl.CostEstimate(flops=60_000_000_000, bytes_accessed=8 << 20, transcendentals=0),
        name="second_factor",
    )(where, inv, *pieces)


def finish_kernel(
    where_ref, inv0_ref, inv1_ref, x01_ref, cols_ref, row0, row1, row2, row3, front_ref, out_ref,
    rows_ref, cols0_ref, cols1_ref,
):
    col, row, shard = where_ref[1], where_ref[2], where_ref[3]
    fill(row, (row0, row1, row2, row3), rows_ref)
    for q in range(COLS):
        for half in range(2):
            at = slice(q * 2 * BLK + half * BLK, q * 2 * BLK + (half + 1) * BLK)
            cols0_ref[at, :] = cols_ref[q, half]
            cols1_ref[at, :] = cols_ref[q, 2 + half]
    r0 = dot_t(rows_ref[:, :PANEL], inv0_ref[...])
    c0 = dot(inv0_ref[...], cols0_ref[...])
    cols0_ref[...] = c0
    r1 = dot_t(rows_ref[:, PANEL:] - dot(r0, x01_ref[...]), inv1_ref[...])
    c1 = dot(inv1_ref[...], cols1_ref[...] - t_dot(x01_ref[...], c0))
    cols1_ref[...] = c1
    update = dot(r0, c0) + dot(r1, c1)
    live = (shard >= ROWS).astype(jnp.float32)
    for slot in range(4, SHARDS):
        rows = slice(slot * BLK, (slot + 1) * BLK)
        out_ref[slot] = (front_ref[slot] - update[rows]) * live
    mine = pl.multiple_of(col * 2 * BLK, 2 * BLK)
    past = (shard >= ROWS // 2).astype(jnp.float32)
    for half in range(2):
        out_ref[half] = cols0_ref[pl.ds(mine + half * BLK, BLK), :]
        out_ref[2 + half] = cols1_ref[pl.ds(mine + half * BLK, BLK), :] * past


def finish(where, inv0, inv1, x01, cols, rows, front):
    return pl.pallas_call(
        finish_kernel,
        out_shape=jax.ShapeDtypeStruct((SHARDS, BLK, WIDE), jnp.float32),
        in_specs=[SMEM] + [VMEM] * 9,
        out_specs=VMEM,
        scratch_shapes=[
            pltpu.VMEM((PANEL, 2 * PANEL), jnp.float32),
            pltpu.VMEM((PANEL, WIDE), jnp.float32),
            pltpu.VMEM((PANEL, WIDE), jnp.float32),
        ],
        compiler_params=params(24),
        name="finish",
    )(where, inv0, inv1, x01, cols, *rows, front)


def swap(x, axis, bit):
    return lax.ppermute(x, axis, [(i, i ^ bit) for i in range(ROWS)])


def to_all(x, axis, count):
    return lax.all_to_all(
        jnp.broadcast_to(x[None], (count, *x.shape)), axis, split_axis=0, concat_axis=0, tiled=True
    )


def exchange(x, axis):
    return lax.all_to_all(x, axis, split_axis=0, concat_axis=0, tiled=True)


def over_rows(x):
    across = swap(x, "row", 2)
    return x, swap(x, "row", 1), across, swap(across, "row", 1)


def local(parent_front, child_schur, index_map):
    sub, row, col = (lax.axis_index(name) for name in ("sub", "row", "col"))
    shard = sub * ROWS + row
    where = jnp.stack([shard // (SHARDS // 2), col, row, shard]).astype(jnp.int32)
    parent = parent_front.reshape(SHARDS, BLK, WIDE)

    crossed = swap(parent[:2, :, TILE:], "row", 2)
    corner = to_all(jnp.where(row < 2, parent[:2, :, :TILE], crossed), "sub", SUBS)[0]
    spread = spread_rows(where, index_map, child_schur)
    tiles = jnp.stack([spread[corner_tile(i)] for i in range(ROWS)])
    tiles = jnp.broadcast_to(tiles[None], (SUBS, ROWS, BLK, TILE)).reshape(SHARDS, BLK, TILE)
    corner = place_corner(where, index_map, exchange(tiles, ("sub", "row")), corner)
    corner = to_all(corner, "col", COLS).reshape(PANEL, TILE)
    inv0 = first_factor(to_all(corner, "row", ROWS))

    chunk = exchange(parent.reshape(SUBS, SHARDS // SUBS, BLK, WIDE), "sub")[0]
    parent_low = to_all(chunk, "sub", SUBS).reshape(SHARDS, BLK, WIDE)
    spread = spread.reshape(SHARDS, 2, BLK, TILE)
    low = jnp.broadcast_to(spread[None, :ROWS], (SUBS, ROWS, 2, BLK, TILE))
    low = exchange(low.reshape(SHARDS, 2, BLK, TILE), ("sub", "row"))
    rows = place(where, index_map, low, parent_low)
    pivots = to_all(rows[2:4], "col", COLS).reshape(SHARDS, BLK, WIDE)
    inv1, x01 = second_factor(where, inv0, over_rows(pivots))

    received = exchange(spread, ("sub", "row"))
    front = place(where, index_map, received, parent)
    cols = to_all(front[:4], "col", COLS)
    out = finish(where, inv0, inv1, x01, cols, over_rows(rows), front)
    return out.reshape(parent_front.shape)


def solution(mesh):
    spec = P(None, "col", None, ("sub", "row"))
    in_specs = (spec, P(("sub", "row", "col"), None), P())
    return jax.shard_map(local, mesh=mesh, in_specs=in_specs, out_specs=spec, check_vma=False)
```

```python
import functools

import jax
import jax.numpy as jnp
from jax import lax
from jax.experimental import pallas as pl
from jax.experimental.pallas import tpu as pltpu
from jax.sharding import PartitionSpec as P

BLK = 16
TILE = 128
STEP = 8
SUBS = 8
ROWS = 4
COLS = 16
SHARDS = SUBS * ROWS
WIDE = 256
PANEL = 512
HIGHEST = lax.Precision.HIGHEST

VMEM = pl.BlockSpec(memory_space=pltpu.VMEM)
SMEM = pl.BlockSpec(memory_space=pltpu.SMEM)


def params(mib):
    return pltpu.CompilerParams(vmem_limit_bytes=mib << 20)


def contract(a, b, dims):
    return lax.dot_general(
        a, b, ((dims[:1], dims[1:]), ((), ())), precision=HIGHEST, preferred_element_type=jnp.float32
    )


def dot(a, b):
    return contract(a, b, (1, 0))


def dot_t(a, b):
    return contract(a, b, (1, 1))


def t_dot(a, b):
    return contract(a, b, (0, 0))


def spread_kernel(where_ref, map_ref, child_ref, out_ref):
    child = where_ref[0]
    out_ref[...] = jnp.zeros_like(out_ref)
    lane_block = lax.broadcasted_iota(jnp.int32, (BLK, TILE), 1) // BLK

    def body(tile, carry):
        rows = child_ref[:, pl.ds(pl.multiple_of(tile * TILE, TILE), TILE)]
        for part in range(TILE // BLK):
            block = map_ref[child, tile * (TILE // BLK) + part]
            place = block % (TILE // BLK)
            target = block // (TILE // BLK)
            shift = (place - part + TILE // BLK) % (TILE // BLK) * BLK
            moved = pltpu.roll(rows, shift, 1)
            out_ref[target] = jnp.where(lane_block == place, moved, out_ref[target])
        return carry

    lax.fori_loop(0, child_ref.shape[1] // TILE, body, 0)


def spread_rows(where, index_map, child):
    return pl.pallas_call(
        spread_kernel,
        out_shape=jax.ShapeDtypeStruct((2 * SHARDS, BLK, TILE), jnp.float32),
        in_specs=[SMEM, SMEM, VMEM],
        out_specs=VMEM,
        compiler_params=params(4),
        name="spread_rows",
    )(where, index_map, child)


def home(group):
    far = group - SUBS
    return (group, 0) if group < SUBS else (far // (SUBS - 1), far % (SUBS - 1) + 1)


def place_kernel(where_ref, map_ref, received_ref, parent_ref, out_ref, dealt_ref):
    col = where_ref[1]

    def body(source, carry):
        child = source // (SHARDS // 2)
        block = map_ref[child, source % (SHARDS // 2) * COLS + col]
        slot = block // (2 * COLS) * 2 + block % 2
        for half in range(2):
            lanes = slice(half * TILE, (half + 1) * TILE)
            out_ref[slot, :, lanes] = parent_ref[slot, :, lanes] + received_ref[source, half]
        return carry

    lax.fori_loop(0, SHARDS, body, 0)
    for group in range(2 * SHARDS):
        owner, number = home(group)
        low = group % 2 * 8
        dealt_ref[owner, number] = out_ref[group // 2, low : low + 8, :]


def place(where, index_map, received, parent):
    return pl.pallas_call(
        place_kernel,
        out_shape=(
            jax.ShapeDtypeStruct((SHARDS, BLK, WIDE), jnp.float32),
            jax.ShapeDtypeStruct((SUBS, 8, 8, WIDE), jnp.float32),
        ),
        in_specs=[SMEM, SMEM, VMEM, VMEM],
        out_specs=(VMEM, VMEM),
        compiler_params=params(6),
        name="place",
    )(where, index_map, received, parent)


def tree_sum(terms):
    while len(terms) > 1:
        terms = [sum(terms[i : i + 2]) for i in range(0, len(terms), 2)]
    return terms[0]


def factor_tile(read, out_ref):
    full = (8, TILE)
    groups = TILE // 8
    sub = lax.broadcasted_iota(jnp.int32, full, 0)
    lane = lax.broadcasted_iota(jnp.int32, full, 1)
    a = [read(h) for h in range(groups)]
    e = [jnp.where(lane == sub + 8 * h, jnp.float32(1), jnp.float32(0)) for h in range(groups)]
    for j in range(0, TILE, STEP):
        g, r = divmod(j, 8)
        col = [
            [jnp.broadcast_to(a[h][:, j + t : j + t + 1], full) for t in range(STEP)]
            for h in range(g, groups)
        ]
        p = [
            [jnp.broadcast_to(col[0][t][r + s : r + s + 1, :], full) for t in range(s + 1)]
            for s in range(STEP)
        ]
        ua = [jnp.broadcast_to(a[g][r + s : r + s + 1, :], full) for s in range(STEP)]
        ue = [jnp.broadcast_to(e[g][r + s : r + s + 1, :], full) for s in range(STEP)]
        rd = [None] * STEP
        low = [[None] * STEP for _ in range(STEP)]
        for t in range(STEP):
            rd[t] = 1.0 / p[t][t]
            for s in range(t + 1, STEP):
                low[s][t] = p[s][t] * rd[t]
            for s in range(t + 1, STEP):
                for q in range(t + 1, s + 1):
                    p[s][q] = p[s][q] - low[s][t] * p[q][t]
            for s in range(t + 1, STEP):
                ua[s] = ua[s] - low[s][t] * ua[t]
                ue[s] = ue[s] - low[s][t] * ue[t]
        for s in range(STEP):
            out_ref[j + s : j + s + 1, :] = (ue[s] * lax.rsqrt(p[s][s]))[0:1, :]
        if j + STEP >= TILE:
            break
        za = [ua[s] * rd[s] for s in range(STEP)]
        ze = [ue[s] * rd[s] for s in range(STEP)]
        for t in range(STEP - 1, 0, -1):
            for s in range(t):
                za[s] = za[s] - low[t][s] * za[t]
                ze[s] = ze[s] - low[t][s] * ze[t]
        for h in range(g, groups):
            if h == g and r + STEP >= 8:
                continue
            c = col[h - g]
            da = tree_sum([c[t] * za[t] for t in range(STEP)])
            de = tree_sum([c[t] * ze[t] for t in range(STEP)])
            if h == g:
                da = jnp.where(sub >= r + STEP, da, 0.0)
                de = jnp.where(sub >= r + STEP, de, 0.0)
            a[h] = a[h] - da
            e[h] = e[h] - de


def invert_factor(m_ref, w_ref, t_ref):
    tiles = m_ref.shape[0] // TILE
    w_ref[...] = jnp.zeros_like(w_ref)

    def body(b, carry):
        low = pl.multiple_of(b * TILE, TILE)
        factor_tile(
            lambda h: m_ref[pl.ds(pl.multiple_of(low + 8 * h, 8), 8), pl.ds(low, TILE)], t_ref
        )
        for c in range(tiles):

            @pl.when(b == c)
            def _():
                lo, hi = c * TILE, (c + 1) * TILE
                t = t_ref[...]
                if c:
                    w_ref[lo:hi, :lo] = dot(t, w_ref[lo:hi, :lo])
                w_ref[lo:hi, lo:hi] = t
                if c + 1 < tiles:
                    x = dot(t, m_ref[lo:hi, hi:])
                    m_ref[hi:, hi:] = m_ref[hi:, hi:] - t_dot(x, x)
                    w_ref[hi:, :hi] = w_ref[hi:, :hi] - t_dot(x, w_ref[lo:hi, :hi])

        return carry

    lax.fori_loop(0, tiles, body, 0)


def fill(row, refs, into, first, last):
    for number, ref in enumerate(refs):
        chunk = (row // 2 ^ number // 2) * 2 + (row % 2 ^ number % 2)

        @pl.when((chunk >= first) & (chunk < last))
        def _():
            low = pl.multiple_of((chunk - first) * WIDE, WIDE)
            for part in range(4):
                for q in range(COLS):
                    at = q * 2 * BLK + part * 8
                    into[at : at + 8, pl.ds(low, WIDE)] = ref[part, q]


def first_kernel(where_ref, own, core, across, both, w_ref, m_ref, t_ref):
    fill(where_ref[2], (own, core, across, both), m_ref, 0, 2)
    invert_factor(m_ref, w_ref, t_ref)


def first_factor(where, pieces):
    return pl.pallas_call(
        first_kernel,
        out_shape=jax.ShapeDtypeStruct((PANEL, PANEL), jnp.float32),
        in_specs=[SMEM] + [VMEM] * 4,
        out_specs=VMEM,
        scratch_shapes=[
            pltpu.VMEM((PANEL, PANEL), jnp.float32),
            pltpu.VMEM((TILE, TILE), jnp.float32),
        ],
        compiler_params=params(10),
        cost_estimate=pl.CostEstimate(flops=60_000_000_000, bytes_accessed=4 << 20, transcendentals=0),
        name="first_factor",
    )(where, *pieces)


def second_kernel(where_ref, inv_ref, *refs):
    upper, lower, (w_ref, x_ref, a_ref, m_ref, t_ref) = refs[:4], refs[4:8], refs[8:]
    fill(where_ref[2], upper, a_ref, 2, 4)
    x_ref[...] = dot(inv_ref[...], a_ref[...])
    fill(where_ref[2], lower, a_ref, 2, 4)
    m_ref[...] = a_ref[...] - t_dot(x_ref[...], x_ref[...])
    invert_factor(m_ref, w_ref, t_ref)


def second_factor(where, inv, upper, lower):
    shape = jax.ShapeDtypeStruct((PANEL, PANEL), jnp.float32)
    return pl.pallas_call(
        second_kernel,
        out_shape=(shape, shape),
        in_specs=[SMEM] + [VMEM] * 9,
        out_specs=(VMEM, VMEM),
        scratch_shapes=[
            pltpu.VMEM((PANEL, PANEL), jnp.float32),
            pltpu.VMEM((PANEL, PANEL), jnp.float32),
            pltpu.VMEM((TILE, TILE), jnp.float32),
        ],
        compiler_params=params(16),
        cost_estimate=pl.CostEstimate(flops=60_000_000_000, bytes_accessed=8 << 20, transcendentals=0),
        name="second_factor",
    )(where, inv, *upper, *lower)


def finish_kernel(
    where_ref, inv0_ref, inv1_ref, x01_ref, cols_ref, row0, row1, row2, row3, front_ref, out_ref,
    rows_ref, cols0_ref, cols1_ref,
):
    col, row, shard = where_ref[1], where_ref[2], where_ref[3]
    for number, ref in enumerate((row0, row1, row2, row3)):
        chunk = (row // 2 ^ number // 2) * 2 + (row % 2 ^ number % 2)
        low = pl.multiple_of(chunk * WIDE, WIDE)
        for group in range(2 * SHARDS):
            rows_ref[group * 8 : (group + 1) * 8, pl.ds(low, WIDE)] = ref[home(group)]
    for q in range(COLS):
        for half in range(2):
            at = slice(q * 2 * BLK + half * BLK, q * 2 * BLK + (half + 1) * BLK)
            cols0_ref[at, :] = cols_ref[q, half]
            cols1_ref[at, :] = cols_ref[q, 2 + half]
    r0 = dot_t(rows_ref[:, :PANEL], inv0_ref[...])
    c0 = dot(inv0_ref[...], cols0_ref[...])
    cols0_ref[...] = c0
    r1 = dot_t(rows_ref[:, PANEL:] - dot(r0, x01_ref[...]), inv1_ref[...])
    c1 = dot(inv1_ref[...], cols1_ref[...] - t_dot(x01_ref[...], c0))
    cols1_ref[...] = c1
    update = dot(r0, c0) + dot(r1, c1)
    live = (shard >= ROWS).astype(jnp.float32)
    for slot in range(4, SHARDS):
        rows = slice(slot * BLK, (slot + 1) * BLK)
        out_ref[slot] = (front_ref[slot] - update[rows]) * live
    mine = pl.multiple_of(col * 2 * BLK, 2 * BLK)
    past = (shard >= ROWS // 2).astype(jnp.float32)
    for half in range(2):
        out_ref[half] = cols0_ref[pl.ds(mine + half * BLK, BLK), :]
        out_ref[2 + half] = cols1_ref[pl.ds(mine + half * BLK, BLK), :] * past


def finish(where, inv0, inv1, x01, cols, rows, front):
    return pl.pallas_call(
        finish_kernel,
        out_shape=jax.ShapeDtypeStruct((SHARDS, BLK, WIDE), jnp.float32),
        in_specs=[SMEM] + [VMEM] * 9,
        out_specs=VMEM,
        scratch_shapes=[
            pltpu.VMEM((PANEL, 2 * PANEL), jnp.float32),
            pltpu.VMEM((PANEL, WIDE), jnp.float32),
            pltpu.VMEM((PANEL, WIDE), jnp.float32),
        ],
        compiler_params=params(24),
        name="finish",
    )(where, inv0, inv1, x01, cols, *rows, front)


def swap(x, axis, bit):
    return lax.ppermute(x, axis, [(i, i ^ bit) for i in range(ROWS)])


def to_all(x, axis, count):
    return lax.all_to_all(
        jnp.broadcast_to(x[None], (count, *x.shape)), axis, split_axis=0, concat_axis=0, tiled=True
    )


def exchange(x, axis):
    return lax.all_to_all(x, axis, split_axis=0, concat_axis=0, tiled=True)


def over_rows(x):
    across = swap(x, "row", 2)
    return x, swap(x, "row", 1), across, swap(across, "row", 1)


def local(parent_front, child_schur, index_map):
    sub, row, col = (lax.axis_index(name) for name in ("sub", "row", "col"))
    shard = sub * ROWS + row
    where = jnp.stack([shard // (SHARDS // 2), col, row, shard]).astype(jnp.int32)
    parent = parent_front.reshape(SHARDS, BLK, WIDE)

    spread = spread_rows(where, index_map, child_schur).reshape(SHARDS, 2, BLK, TILE)
    front, dealt = place(where, index_map, exchange(spread, ("sub", "row")), parent)

    chunk = exchange(dealt, "sub")[0]
    pivots = to_all(chunk[0], ("sub", "col"), SUBS * COLS).reshape(2, 4, COLS, 8, WIDE)
    upper = over_rows(pivots[0])
    inv0 = first_factor(where, upper)

    chunk, _ = lax.optimization_barrier((chunk, pivots))
    rows, _ = lax.optimization_barrier((to_all(chunk, "sub", SUBS), inv0))
    rows = over_rows(rows)
    inv1, x01 = second_factor(where, inv0, upper, over_rows(pivots[1]))

    top, _ = lax.optimization_barrier((front[:4], inv0))
    cols = to_all(top, "col", COLS)
    out = finish(where, inv0, inv1, x01, cols, rows, front)
    return out.reshape(parent_front.shape)


def solution(mesh):
    spec = P(None, "col", None, ("sub", "row"))
    in_specs = (spec, P(("sub", "row", "col"), None), P())
    return jax.shard_map(local, mesh=mesh, in_specs=in_specs, out_specs=spec, check_vma=False)
```

```python
import functools

import jax
import jax.numpy as jnp
from jax import lax
from jax.experimental import pallas as pl
from jax.experimental.pallas import tpu as pltpu
from jax.sharding import PartitionSpec as P

BLK = 16
TILE = 128
STEP = 8
SUBS = 8
ROWS = 4
COLS = 16
SHARDS = SUBS * ROWS
WIDE = 256
PANEL = 512
TOP = 4
HIGHEST = lax.Precision.HIGHEST

VMEM = pl.BlockSpec(memory_space=pltpu.VMEM)
SMEM = pl.BlockSpec(memory_space=pltpu.SMEM)


def params(mib):
    return pltpu.CompilerParams(vmem_limit_bytes=mib << 20)


def contract(a, b, dims):
    return lax.dot_general(
        a, b, ((dims[:1], dims[1:]), ((), ())), precision=HIGHEST, preferred_element_type=jnp.float32
    )


def split(a):
    high = a.astype(jnp.bfloat16)
    return high, (a - high.astype(jnp.float32)).astype(jnp.bfloat16)


def contract_split(a, b, dims):
    def product(x, y):
        return lax.dot_general(
            x, y, ((dims[:1], dims[1:]), ((), ())), preferred_element_type=jnp.float32
        )

    return product(a[0], b[1]) + product(a[1], b[0]) + product(a[0], b[0])


def dot(a, b):
    return contract(a, b, (1, 0))


def dot_t(a, b):
    return contract(a, b, (1, 1))


def t_dot(a, b):
    return contract(a, b, (0, 0))


def spread_kernel(where_ref, map_ref, child_ref, out_ref, low_ref):
    child = where_ref[0]
    out_ref[...] = jnp.zeros_like(out_ref)
    lane_block = lax.broadcasted_iota(jnp.int32, (BLK, TILE), 1) // BLK

    def body(tile, carry):
        rows = child_ref[:, pl.ds(pl.multiple_of(tile * TILE, TILE), TILE)]
        for part in range(TILE // BLK):
            block = map_ref[child, tile * (TILE // BLK) + part]
            place = block % (TILE // BLK)
            target = block // (TILE // BLK)
            shift = (place - part + TILE // BLK) % (TILE // BLK) * BLK
            moved = pltpu.roll(rows, shift, 1)
            out_ref[target] = jnp.where(lane_block == place, moved, out_ref[target])
        return carry

    lax.fori_loop(0, child_ref.shape[1] // TILE, body, 0)
    for sub in range(SUBS):
        low_ref[sub] = out_ref[: 2 * ROWS]


def spread_rows(where, index_map, child):
    return pl.pallas_call(
        spread_kernel,
        out_shape=(
            jax.ShapeDtypeStruct((2 * SHARDS, BLK, TILE), jnp.float32),
            jax.ShapeDtypeStruct((SUBS, 2 * ROWS, BLK, TILE), jnp.float32),
        ),
        in_specs=[SMEM, SMEM, VMEM],
        out_specs=(VMEM, VMEM),
        compiler_params=params(4),
        name="spread_rows",
    )(where, index_map, child)


def each_source(where_ref, map_ref, use):
    col = where_ref[1]

    def body(source, carry):
        child = source // (SHARDS // 2)
        block = map_ref[child, source % (SHARDS // 2) * COLS + col]
        use(source, block // (2 * COLS) * 2 + block % 2)
        return carry

    lax.fori_loop(0, SHARDS, body, 0)


def add_block(out_ref, slot, parent, received_ref, source):
    for half in range(2):
        lanes = slice(half * TILE, (half + 1) * TILE)
        out_ref[slot, :, lanes] = parent[:, lanes] + received_ref[source, half]


def place_kernel(where_ref, map_ref, received_ref, parent_ref, out_ref, top_ref):
    def use(source, slot):
        add_block(out_ref, slot, parent_ref[slot], received_ref, source)

    each_source(where_ref, map_ref, use)
    for q in range(COLS):
        top_ref[q] = out_ref[:TOP]


def place_top_kernel(where_ref, map_ref, received_ref, parent_ref, top_ref, out_ref):
    def use(source, slot):
        @pl.when(slot < TOP)
        def _():
            add_block(out_ref, slot, parent_ref[slot], received_ref, source)

    each_source(where_ref, map_ref, use)
    for q in range(COLS):
        top_ref[q] = out_ref[...]


def place_rest_kernel(where_ref, map_ref, received_ref, parent_ref, top_ref, out_ref):
    def use(source, slot):
        @pl.when(slot >= TOP)
        def _():
            add_block(out_ref, slot, parent_ref[slot - TOP], received_ref, source)

    each_source(where_ref, map_ref, use)
    out_ref[:TOP] = top_ref[0]


FRONT = jax.ShapeDtypeStruct((SHARDS, BLK, WIDE), jnp.float32)
TOPS = jax.ShapeDtypeStruct((COLS, TOP, BLK, WIDE), jnp.float32)


def call(kernel, out_shape, operands, mib, scratch=(), flops=None):
    cost = flops and pl.CostEstimate(flops=flops, bytes_accessed=4 << 20, transcendentals=0)
    return pl.pallas_call(
        kernel,
        out_shape=out_shape,
        in_specs=[SMEM, SMEM] + [VMEM] * (len(operands) - 2),
        out_specs=jax.tree.map(lambda _: VMEM, out_shape),
        scratch_shapes=list(scratch),
        compiler_params=params(mib),
        cost_estimate=cost,
        name=kernel.__name__.removesuffix("_kernel"),
    )(*operands)


def tree_sum(terms):
    while len(terms) > 1:
        terms = [sum(terms[i : i + 2]) for i in range(0, len(terms), 2)]
    return terms[0]


def factor_tile(read, out_ref):
    full = (8, TILE)
    groups = TILE // 8
    sub = lax.broadcasted_iota(jnp.int32, full, 0)
    lane = lax.broadcasted_iota(jnp.int32, full, 1)
    a = [read(h) for h in range(groups)]
    e = [jnp.where(lane == sub + 8 * h, jnp.float32(1), jnp.float32(0)) for h in range(groups)]
    for j in range(0, TILE, STEP):
        g, r = divmod(j, 8)
        col = [
            [jnp.broadcast_to(a[h][:, j + t : j + t + 1], full) for t in range(STEP)]
            for h in range(g, groups)
        ]
        p = [
            [jnp.broadcast_to(col[0][t][r + s : r + s + 1, :], full) for t in range(s + 1)]
            for s in range(STEP)
        ]
        ua = [jnp.broadcast_to(a[g][r + s : r + s + 1, :], full) for s in range(STEP)]
        ue = [jnp.broadcast_to(e[g][r + s : r + s + 1, :], full) for s in range(STEP)]
        rd = [None] * STEP
        low = [[None] * STEP for _ in range(STEP)]
        for t in range(STEP):
            rd[t] = 1.0 / p[t][t]
            for s in range(t + 1, STEP):
                low[s][t] = p[s][t] * rd[t]
            for s in range(t + 1, STEP):
                for q in range(t + 1, s + 1):
                    p[s][q] = p[s][q] - low[s][t] * p[q][t]
            for s in range(t + 1, STEP):
                ua[s] = ua[s] - low[s][t] * ua[t]
                ue[s] = ue[s] - low[s][t] * ue[t]
        for s in range(STEP):
            out_ref[j + s : j + s + 1, :] = (ue[s] * lax.rsqrt(p[s][s]))[0:1, :]
        if j + STEP >= TILE:
            break
        za = [ua[s] * rd[s] for s in range(STEP)]
        ze = [ue[s] * rd[s] for s in range(STEP)]
        for t in range(STEP - 1, 0, -1):
            for s in range(t):
                za[s] = za[s] - low[t][s] * za[t]
                ze[s] = ze[s] - low[t][s] * ze[t]
        for h in range(g, groups):
            if h == g and r + STEP >= 8:
                continue
            c = col[h - g]
            da = tree_sum([c[t] * za[t] for t in range(STEP)])
            de = tree_sum([c[t] * ze[t] for t in range(STEP)])
            if h == g:
                da = jnp.where(sub >= r + STEP, da, 0.0)
                de = jnp.where(sub >= r + STEP, de, 0.0)
            a[h] = a[h] - da
            e[h] = e[h] - de


def invert_factor(m_ref, w_ref, t_ref):
    tiles = m_ref.shape[0] // TILE
    w_ref[...] = jnp.zeros_like(w_ref)

    def body(b, carry):
        low = pl.multiple_of(b * TILE, TILE)
        factor_tile(
            lambda h: m_ref[pl.ds(pl.multiple_of(low + 8 * h, 8), 8), pl.ds(low, TILE)], t_ref
        )
        for c in range(tiles):

            @pl.when(b == c)
            def _():
                lo, hi = c * TILE, (c + 1) * TILE
                t = t_ref[...]
                if c:
                    w_ref[lo:hi, :lo] = dot(t, w_ref[lo:hi, :lo])
                w_ref[lo:hi, lo:hi] = t
                if c + 1 < tiles:
                    x = dot(t, m_ref[lo:hi, hi:])
                    m_ref[hi:, hi:] = m_ref[hi:, hi:] - t_dot(x, x)
                    w_ref[hi:, :hi] = w_ref[hi:, :hi] - t_dot(x, w_ref[lo:hi, :hi])

        return carry

    lax.fori_loop(0, tiles, body, 0)


def fill(row, refs, into, first, last):
    for number, ref in enumerate(refs):
        chunk = (row // 2 ^ number // 2) * 2 + (row % 2 ^ number % 2)

        @pl.when((chunk >= first) & (chunk < last))
        def _():
            low = pl.multiple_of((chunk - first) * WIDE, WIDE)
            for q in range(COLS):
                for half in range(2):
                    at = (2 * q + half) * BLK
                    into[at : at + BLK, pl.ds(low, WIDE)] = ref[q, half]


def first_kernel(where_ref, own, core, across, both, w_ref, m_ref, t_ref):
    fill(where_ref[2], (own, core, across, both), m_ref, 0, 2)
    invert_factor(m_ref, w_ref, t_ref)


def first_factor(where, pieces):
    return pl.pallas_call(
        first_kernel,
        out_shape=jax.ShapeDtypeStruct((PANEL, PANEL), jnp.float32),
        in_specs=[SMEM] + [VMEM] * 4,
        out_specs=VMEM,
        scratch_shapes=[
            pltpu.VMEM((PANEL, PANEL), jnp.float32),
            pltpu.VMEM((TILE, TILE), jnp.float32),
        ],
        compiler_params=params(10),
        cost_estimate=pl.CostEstimate(flops=60_000_000_000, bytes_accessed=4 << 20, transcendentals=0),
        name="first_factor",
    )(where, *pieces)


def second_kernel(where_ref, inv_ref, *refs):
    upper, lower, (w_ref, x_ref, a_ref, m_ref, t_ref) = refs[:4], refs[4:8], refs[8:]
    fill(where_ref[2], upper, a_ref, 2, 4)
    x_ref[...] = dot(inv_ref[...], a_ref[...])
    fill(where_ref[2], lower, a_ref, 2, 4)
    m_ref[...] = a_ref[...] - t_dot(x_ref[...], x_ref[...])
    invert_factor(m_ref, w_ref, t_ref)


def second_factor(where, inv, upper, lower):
    shape = jax.ShapeDtypeStruct((PANEL, PANEL), jnp.float32)
    return pl.pallas_call(
        second_kernel,
        out_shape=(shape, shape),
        in_specs=[SMEM] + [VMEM] * 9,
        out_specs=(VMEM, VMEM),
        scratch_shapes=[
            pltpu.VMEM((PANEL, PANEL), jnp.float32),
            pltpu.VMEM((PANEL, PANEL), jnp.float32),
            pltpu.VMEM((TILE, TILE), jnp.float32),
        ],
        compiler_params=params(16),
        cost_estimate=pl.CostEstimate(flops=60_000_000_000, bytes_accessed=8 << 20, transcendentals=0),
        name="second_factor",
    )(where, inv, *upper, *lower)


def finish_kernel(
    where_ref, inv0_ref, inv1_ref, x01_ref, cols_ref, row0, row1, row2, row3, front_ref, out_ref,
    rows_ref, cols0_ref, cols1_ref,
):
    col, row, shard = where_ref[1], where_ref[2], where_ref[3]
    for number, ref in enumerate((row0, row1, row2, row3)):
        chunk = (row // 2 ^ number // 2) * 2 + (row % 2 ^ number % 2)
        low = pl.multiple_of(chunk * WIDE, WIDE)
        for slot in range(SHARDS):
            rows_ref[slot * BLK : (slot + 1) * BLK, pl.ds(low, WIDE)] = ref[slot]
    for q in range(COLS):
        for half in range(2):
            at = slice(q * 2 * BLK + half * BLK, q * 2 * BLK + (half + 1) * BLK)
            cols0_ref[at, :] = cols_ref[q, half]
            cols1_ref[at, :] = cols_ref[q, 2 + half]
    inv0, inv1, x01 = split(inv0_ref[...]), split(inv1_ref[...]), split(x01_ref[...])
    r0 = split(contract_split(split(rows_ref[:, :PANEL]), inv0, (1, 1)))
    c0 = contract_split(inv0, split(cols0_ref[...]), (1, 0))
    cols0_ref[...] = c0
    c0 = split(c0)
    r1 = split(rows_ref[:, PANEL:] - contract_split(r0, x01, (1, 0)))
    r1 = split(contract_split(r1, inv1, (1, 1)))
    c1 = split(cols1_ref[...] - contract_split(x01, c0, (0, 0)))
    c1 = contract_split(inv1, c1, (1, 0))
    cols1_ref[...] = c1
    update = contract_split(r0, c0, (1, 0)) + contract_split(r1, split(c1), (1, 0))
    live = (shard >= ROWS).astype(jnp.float32)
    for slot in range(4, SHARDS):
        rows = slice(slot * BLK, (slot + 1) * BLK)
        out_ref[slot] = (front_ref[slot] - update[rows]) * live
    mine = pl.multiple_of(col * 2 * BLK, 2 * BLK)
    past = (shard >= ROWS // 2).astype(jnp.float32)
    for half in range(2):
        out_ref[half] = cols0_ref[pl.ds(mine + half * BLK, BLK), :]
        out_ref[2 + half] = cols1_ref[pl.ds(mine + half * BLK, BLK), :] * past


def finish(where, inv0, inv1, x01, cols, rows, front):
    return pl.pallas_call(
        finish_kernel,
        out_shape=jax.ShapeDtypeStruct((SHARDS, BLK, WIDE), jnp.float32),
        in_specs=[SMEM] + [VMEM] * 9,
        out_specs=VMEM,
        scratch_shapes=[
            pltpu.VMEM((PANEL, 2 * PANEL), jnp.float32),
            pltpu.VMEM((PANEL, WIDE), jnp.float32),
            pltpu.VMEM((PANEL, WIDE), jnp.float32),
        ],
        compiler_params=params(24),
        name="finish",
    )(where, inv0, inv1, x01, cols, *rows, front)


def swap(x, axis, bit):
    return lax.ppermute(x, axis, [(i, i ^ bit) for i in range(ROWS)])


def to_all(x, axis, count):
    return lax.all_to_all(
        jnp.broadcast_to(x[None], (count, *x.shape)), axis, split_axis=0, concat_axis=0, tiled=True
    )


def exchange(x, axis):
    return lax.all_to_all(x, axis, split_axis=0, concat_axis=0, tiled=True)


def over_rows(x):
    across = swap(x, "row", 2)
    return x, swap(x, "row", 1), across, swap(across, "row", 1)


def from_first(x, sub):
    for step in (4, 2, 1):
        pairs = [(i, i + step) for i in range(0, SUBS, 2 * step)]
        got = lax.ppermute(x, "sub", pairs)
        x = jnp.where(sub % (2 * step) == step, got, x)
    return x


def local(parent_front, child_schur, index_map):
    sub, row, col = (lax.axis_index(name) for name in ("sub", "row", "col"))
    shard = sub * ROWS + row
    where = jnp.stack([shard // (SHARDS // 2), col, row, shard]).astype(jnp.int32)
    parent = parent_front.reshape(SHARDS, BLK, WIDE)
    parent_top = from_first(parent[:TOP], sub)
    parent_rest = from_first(parent[TOP:], sub)

    spread, low = spread_rows(where, index_map, child_schur)
    low = exchange(low.reshape(SHARDS, 2, BLK, TILE), ("sub", "row"))
    tops, _ = call(
        place_top_kernel,
        (TOPS, jax.ShapeDtypeStruct((TOP, BLK, WIDE), jnp.float32)),
        (where, index_map, low, parent_top),
        6,
    )
    pivots = exchange(tops, "col")
    rows = call(place_rest_kernel, FRONT, (where, index_map, low, parent_rest, tops), 6)
    rows = over_rows(rows)
    upper = over_rows(pivots[:, :2])
    lower = over_rows(pivots[:, 2:])
    inv0 = first_factor(where, upper)

    spread, _ = lax.optimization_barrier((spread.reshape(SHARDS, 2, BLK, TILE), pivots))
    received, _ = lax.optimization_barrier((exchange(spread, ("sub", "row")), inv0))
    front, tops = call(place_kernel, (FRONT, TOPS), (where, index_map, received, parent), 6)
    inv1, x01 = second_factor(where, inv0, upper, lower)
    cols = exchange(tops, "col")
    out = finish(where, inv0, inv1, x01, cols, rows, front)
    return out.reshape(parent_front.shape)


def solution(mesh):
    spec = P(None, "col", None, ("sub", "row"))
    in_specs = (spec, P(("sub", "row", "col"), None), P())
    return jax.shard_map(local, mesh=mesh, in_specs=in_specs, out_specs=spec, check_vma=False)
```

```python
import functools

import jax
import jax.numpy as jnp
from jax import lax
from jax.experimental import pallas as pl
from jax.experimental.pallas import tpu as pltpu
from jax.sharding import PartitionSpec as P

BLK = 16
TILE = 128
STEP = 8
SUBS = 8
ROWS = 4
COLS = 16
SHARDS = SUBS * ROWS
WIDE = 256
PANEL = 512
TOP = 4

VMEM = pl.BlockSpec(memory_space=pltpu.VMEM)
SMEM = pl.BlockSpec(memory_space=pltpu.SMEM)
HBM = pl.BlockSpec(memory_space=pl.ANY)


def params(mib):
    return pltpu.CompilerParams(vmem_limit_bytes=mib << 20)


def split(a):
    high = a.astype(jnp.bfloat16)
    return high, (a - high.astype(jnp.float32)).astype(jnp.bfloat16)


def contract_split(a, b, dims):
    def product(x, y):
        return lax.dot_general(
            x, y, ((dims[:1], dims[1:]), ((), ())), preferred_element_type=jnp.float32
        )

    return product(a[0], b[1]) + product(a[1], b[0]) + product(a[0], b[0])


def spread_kernel(where_ref, map_ref, child_ref, out_ref):
    child = where_ref[0]
    out_ref[...] = jnp.zeros_like(out_ref)
    lane_block = lax.broadcasted_iota(jnp.int32, (BLK, TILE), 1) // BLK

    def body(tile, carry):
        rows = child_ref[:, pl.ds(pl.multiple_of(tile * TILE, TILE), TILE)]
        for part in range(TILE // BLK):
            block = map_ref[child, tile * (TILE // BLK) + part]
            place = block % (TILE // BLK)
            target = block // (TILE // BLK)
            shift = (place - part + TILE // BLK) % (TILE // BLK) * BLK
            moved = pltpu.roll(rows, shift, 1)
            out_ref[target] = jnp.where(lane_block == place, moved, out_ref[target])
        return carry

    lax.fori_loop(0, child_ref.shape[1] // TILE, body, 0)


def spread_low_kernel(where_ref, map_ref, child_ref, out_ref):
    child = where_ref[0]
    count = 2 * ROWS
    out_ref[0] = jnp.zeros_like(out_ref[0])
    lane_block = lax.broadcasted_iota(jnp.int32, (BLK, TILE), 1) // BLK

    def body(tile, carry):
        for part in range(TILE // BLK):
            block = map_ref[child, tile * (TILE // BLK) + part]
            target = block // (TILE // BLK)

            @pl.when(target < count)
            def _():
                place = block % (TILE // BLK)
                rows = child_ref[:, pl.ds(pl.multiple_of(tile * TILE, TILE), TILE)]
                shift = (place - part + TILE // BLK) % (TILE // BLK) * BLK
                moved = pltpu.roll(rows, shift, 1)
                out_ref[0, target] = jnp.where(lane_block == place, moved, out_ref[0, target])

        return carry

    lax.fori_loop(0, child_ref.shape[1] // TILE, body, 0)
    for sub in range(1, SUBS):
        out_ref[sub] = out_ref[0]


def each_source(where_ref, map_ref, use):
    col = where_ref[1]

    def body(source, carry):
        child = source // (SHARDS // 2)
        block = map_ref[child, source % (SHARDS // 2) * COLS + col]
        use(source, block // (2 * COLS) * 2 + block % 2)
        return carry

    lax.fori_loop(0, SHARDS, body, 0)


def add_block(out_ref, slot, parent, received_ref, source):
    for half in range(2):
        lanes = slice(half * TILE, (half + 1) * TILE)
        out_ref[slot, :, lanes] = parent[:, lanes] + received_ref[source, half]


def place_kernel(where_ref, map_ref, received_ref, parent_ref, out_ref, top_ref):
    def use(source, slot):
        add_block(out_ref, slot, parent_ref[slot], received_ref, source)

    each_source(where_ref, map_ref, use)
    for q in range(COLS):
        top_ref[q] = out_ref[:TOP]


def place_top_kernel(where_ref, map_ref, received_ref, parent_ref, top_ref, out_ref):
    def use(source, slot):
        @pl.when(slot < TOP)
        def _():
            add_block(out_ref, slot, parent_ref[slot], received_ref, source)

    each_source(where_ref, map_ref, use)
    for q in range(COLS):
        top_ref[q] = out_ref[...]


def place_rest_kernel(where_ref, map_ref, received_ref, parent_ref, top_ref, pivots_ref, out_ref):
    def use(source, slot):
        @pl.when(slot >= TOP)
        def _():
            add_block(out_ref, SHARDS + slot, parent_ref[slot - TOP], received_ref, source)

    each_source(where_ref, map_ref, use)
    for q in range(COLS):
        for half in range(2):
            out_ref[2 * q + half] = pivots_ref[q, 2 + half]
    out_ref[SHARDS : SHARDS + TOP] = top_ref[0]


FRONT = jax.ShapeDtypeStruct((SHARDS, BLK, WIDE), jnp.float32)
TOPS = jax.ShapeDtypeStruct((COLS, TOP, BLK, WIDE), jnp.float32)


def call(kernel, out_shape, operands, mib, scratch=(), flops=None):
    cost = flops and pl.CostEstimate(flops=flops, bytes_accessed=4 << 20, transcendentals=0)
    return pl.pallas_call(
        kernel,
        out_shape=out_shape,
        in_specs=[SMEM, SMEM] + [VMEM] * (len(operands) - 2),
        out_specs=jax.tree.map(lambda _: VMEM, out_shape),
        scratch_shapes=list(scratch),
        compiler_params=params(mib),
        cost_estimate=cost,
        name=kernel.__name__.removesuffix("_kernel"),
    )(*operands)


def tree_sum(terms):
    while len(terms) > 1:
        terms = [sum(terms[i : i + 2]) for i in range(0, len(terms), 2)]
    return terms[0]


def factor_tile(read, out_ref):
    full = (8, TILE)
    groups = TILE // 8
    sub = lax.broadcasted_iota(jnp.int32, full, 0)
    lane = lax.broadcasted_iota(jnp.int32, full, 1)
    a = [read(h) for h in range(groups)]
    e = [jnp.where(lane == sub + 8 * h, jnp.float32(1), jnp.float32(0)) for h in range(groups)]
    for j in range(0, TILE, STEP):
        g, r = divmod(j, 8)
        col = [
            [jnp.broadcast_to(a[h][:, j + t : j + t + 1], full) for t in range(STEP)]
            for h in range(g, groups)
        ]
        p = [
            [jnp.broadcast_to(col[0][t][r + s : r + s + 1, :], full) for t in range(s + 1)]
            for s in range(STEP)
        ]
        ua = [jnp.broadcast_to(a[g][r + s : r + s + 1, :], full) for s in range(STEP)]
        ue = [jnp.broadcast_to(e[g][r + s : r + s + 1, :], full) for s in range(STEP)]
        rd = [None] * STEP
        low = [[None] * STEP for _ in range(STEP)]
        for t in range(STEP):
            rd[t] = 1.0 / p[t][t]
            for s in range(t + 1, STEP):
                low[s][t] = p[s][t] * rd[t]
            for s in range(t + 1, STEP):
                for q in range(t + 1, s + 1):
                    p[s][q] = p[s][q] - low[s][t] * p[q][t]
            for s in range(t + 1, STEP):
                ua[s] = ua[s] - low[s][t] * ua[t]
                ue[s] = ue[s] - low[s][t] * ue[t]
        for s in range(STEP):
            out_ref[j + s : j + s + 1, :] = (ue[s] * lax.rsqrt(p[s][s]))[0:1, :]
        if j + STEP >= TILE:
            break
        za = [ua[s] * rd[s] for s in range(STEP)]
        ze = [ue[s] * rd[s] for s in range(STEP)]
        for t in range(STEP - 1, 0, -1):
            for s in range(t):
                za[s] = za[s] - low[t][s] * za[t]
                ze[s] = ze[s] - low[t][s] * ze[t]
        for h in range(g, groups):
            if h == g and r + STEP >= 8:
                continue
            c = col[h - g]
            da = tree_sum([c[t] * za[t] for t in range(STEP)])
            de = tree_sum([c[t] * ze[t] for t in range(STEP)])
            if h == g:
                da = jnp.where(sub >= r + STEP, da, 0.0)
                de = jnp.where(sub >= r + STEP, de, 0.0)
            a[h] = a[h] - da
            e[h] = e[h] - de


def multiply(a, b, dims):
    return contract_split(split(a), split(b), dims)


def invert_factor(m_ref, w_ref, t_ref):
    tiles = m_ref.shape[0] // TILE
    w_ref[...] = jnp.zeros_like(w_ref)

    def body(b, carry):
        low = pl.multiple_of(b * TILE, TILE)
        factor_tile(
            lambda h: m_ref[pl.ds(pl.multiple_of(low + 8 * h, 8), 8), pl.ds(low, TILE)], t_ref
        )
        for c in range(tiles):

            @pl.when(b == c)
            def _():
                lo, hi = c * TILE, (c + 1) * TILE
                t = t_ref[...]
                if c:
                    w_ref[lo:hi, :lo] = multiply(t, w_ref[lo:hi, :lo], (1, 0))
                w_ref[lo:hi, lo:hi] = t
                if c + 1 < tiles:
                    x = multiply(t, m_ref[lo:hi, hi:], (1, 0))
                    m_ref[hi:, hi:] = m_ref[hi:, hi:] - multiply(x, x, (0, 0))
                    w_ref[hi:, :hi] = w_ref[hi:, :hi] - multiply(x, w_ref[lo:hi, :hi], (0, 0))

        return carry

    lax.fori_loop(0, tiles, body, 0)


def chunk_of(row, number):
    return (row // 2 ^ number // 2) * 2 + (row % 2 ^ number % 2)


def each_chunk(row, refs, use, first=0, last=ROWS):
    for number, ref in enumerate(refs):
        chunk = chunk_of(row, number)

        @pl.when((chunk >= first) & (chunk < last))
        def _():
            use(number, ref, pl.ds(pl.multiple_of((chunk - first) * WIDE, WIDE), WIDE))


def first_kernel(where_ref, own, core, across, both, w_ref, m_ref, t_ref, sems):
    def copy(number, ref, lanes):
        return pltpu.make_async_copy(ref, m_ref.at[:, lanes], sems.at[number])

    row, refs = where_ref[2], (own, core, across, both)
    each_chunk(row, refs, lambda *at: copy(*at).start(), 0, 2)
    each_chunk(row, refs, lambda *at: copy(*at).wait(), 0, 2)
    invert_factor(m_ref, w_ref, t_ref)


def square():
    return pltpu.VMEM((PANEL, PANEL), jnp.float32)


def first_factor(where, pieces):
    return pl.pallas_call(
        first_kernel,
        out_shape=jax.ShapeDtypeStruct((PANEL, PANEL), jnp.float32),
        in_specs=[SMEM] + [HBM] * 4,
        out_specs=VMEM,
        scratch_shapes=[
            square(),
            pltpu.VMEM((TILE, TILE), jnp.float32),
            pltpu.SemaphoreType.DMA((4,)),
        ],
        compiler_params=params(10),
        cost_estimate=pl.CostEstimate(flops=60_000_000_000, bytes_accessed=4 << 20, transcendentals=0),
        name="first_factor",
    )(where, *pieces)


def second_kernel(where_ref, inv_hbm, *refs):
    upper, lower, refs = refs[:4], refs[4:8], refs[8:]
    w_hbm, x_hbm, inv_ref, a_ref, m_ref, w_ref, x_ref, t_ref, sems = refs

    def copy_upper(number, ref, lanes):
        return pltpu.make_async_copy(ref, a_ref.at[:, lanes], sems.at[number])

    def copy_lower(number, ref, lanes):
        rows = ref.at[pl.ds(0, PANEL), :]
        return pltpu.make_async_copy(rows, m_ref.at[:, lanes], sems.at[4 + number])

    row = where_ref[2]
    inv = pltpu.make_async_copy(inv_hbm, inv_ref, sems.at[8])
    inv.start()
    each_chunk(row, upper, lambda *at: copy_upper(*at).start(), 2, 4)
    each_chunk(row, lower, lambda *at: copy_lower(*at).start(), 2, 4)
    inv.wait()
    each_chunk(row, upper, lambda *at: copy_upper(*at).wait(), 2, 4)
    x_ref[...] = multiply(inv_ref[...], a_ref[...], (1, 0))
    out = pltpu.make_async_copy(x_ref, x_hbm, sems.at[9])
    out.start()
    x = x_ref[...]
    each_chunk(row, lower, lambda *at: copy_lower(*at).wait(), 2, 4)
    m_ref[...] = m_ref[...] - multiply(x, x, (0, 0))
    invert_factor(m_ref, w_ref, t_ref)
    last = pltpu.make_async_copy(w_ref, w_hbm, sems.at[10])
    last.start()
    out.wait()
    last.wait()


def second_factor(where, inv, upper, lower):
    shape = jax.ShapeDtypeStruct((PANEL, PANEL), jnp.float32)
    return pl.pallas_call(
        second_kernel,
        out_shape=(shape, shape),
        in_specs=[SMEM] + [HBM] * 9,
        out_specs=(HBM, HBM),
        scratch_shapes=[
            square(), square(), square(), square(), square(),
            pltpu.VMEM((TILE, TILE), jnp.float32),
            pltpu.SemaphoreType.DMA((11,)),
        ],
        compiler_params=params(20),
        cost_estimate=pl.CostEstimate(flops=60_000_000_000, bytes_accessed=8 << 20, transcendentals=0),
        name="second_factor",
    )(where, inv, *upper, *lower)


def finish_kernel(
    where_ref, inv0_hbm, inv1_hbm, x01_hbm, cols_hbm, row0, row1, row2, row3, front_hbm, out_ref,
    inv0_ref, inv1_ref, x01_ref, rows_ref, cols0_ref, cols1_ref, front_ref, sems,
):
    col, row, shard = where_ref[1], where_ref[2], where_ref[3]
    refs = (row0, row1, row2, row3)

    def copy_rows(number, ref, lanes):
        return pltpu.make_async_copy(
            ref.at[pl.ds(PANEL, PANEL), :], rows_ref.at[:, lanes], sems.at[number]
        )

    copies = [
        (inv0_hbm, inv0_ref),
        (cols_hbm.at[:, pl.ds(0, 2 * BLK), :], cols0_ref),
        (cols_hbm.at[:, pl.ds(2 * BLK, 2 * BLK), :], cols1_ref),
        (x01_hbm, x01_ref),
        (inv1_hbm, inv1_ref),
        (front_hbm, front_ref),
    ]
    copies = [
        pltpu.make_async_copy(source, target, sems.at[4 + i])
        for i, (source, target) in enumerate(copies)
    ]
    each_chunk(row, refs, lambda *at: copy_rows(*at).start())
    for copy in copies:
        copy.start()
    each_chunk(row, refs, lambda *at: copy_rows(*at).wait())
    for copy in copies:
        copy.wait()
    inv0, inv1, x01 = split(inv0_ref[...]), split(inv1_ref[...]), split(x01_ref[...])
    r0 = split(contract_split(split(rows_ref[:, :PANEL]), inv0, (1, 1)))
    c0 = contract_split(inv0, split(cols0_ref[...].reshape(PANEL, WIDE)), (1, 0))
    cols0_ref[...] = c0.reshape(cols0_ref.shape)
    c0 = split(c0)
    r1 = split(rows_ref[:, PANEL:] - contract_split(r0, x01, (1, 0)))
    r1 = split(contract_split(r1, inv1, (1, 1)))
    c1 = split(cols1_ref[...].reshape(PANEL, WIDE) - contract_split(x01, c0, (0, 0)))
    c1 = contract_split(inv1, c1, (1, 0))
    cols1_ref[...] = c1.reshape(cols1_ref.shape)
    update = contract_split(r0, c0, (1, 0)) + contract_split(r1, split(c1), (1, 0))
    live = (shard >= ROWS).astype(jnp.float32)
    for slot in range(TOP, SHARDS):
        rows = slice(slot * BLK, (slot + 1) * BLK)
        out_ref[slot] = (front_ref[slot] - update[rows]) * live
    past = (shard >= ROWS // 2).astype(jnp.float32)
    for half in range(2):
        rows = slice(half * BLK, (half + 1) * BLK)
        out_ref[half] = cols0_ref[col, rows, :]
        out_ref[2 + half] = cols1_ref[col, rows, :] * past


def finish(where, inv0, inv1, x01, cols, rows, front):
    return pl.pallas_call(
        finish_kernel,
        out_shape=FRONT,
        in_specs=[SMEM] + [HBM] * 9,
        out_specs=VMEM,
        scratch_shapes=[
            square(), square(), square(),
            pltpu.VMEM((PANEL, 2 * PANEL), jnp.float32),
            pltpu.VMEM((COLS, 2 * BLK, WIDE), jnp.float32),
            pltpu.VMEM((COLS, 2 * BLK, WIDE), jnp.float32),
            pltpu.VMEM((SHARDS, BLK, WIDE), jnp.float32),
            pltpu.SemaphoreType.DMA((10,)),
        ],
        compiler_params=params(28),
        name="finish",
    )(where, inv0, inv1, x01, cols, *rows, front)


def swap(x, axis, bit):
    return lax.ppermute(x, axis, [(i, i ^ bit) for i in range(ROWS)])


def to_all(x, axis, count):
    return lax.all_to_all(
        jnp.broadcast_to(x[None], (count, *x.shape)), axis, split_axis=0, concat_axis=0, tiled=True
    )


def exchange(x, axis):
    return lax.all_to_all(x, axis, split_axis=0, concat_axis=0, tiled=True)


def over_rows(x):
    across = swap(x, "row", 2)
    return x, swap(x, "row", 1), across, swap(across, "row", 1)


def from_first(x, sub):
    for step in (4, 2, 1):
        pairs = [(i, i + step) for i in range(0, SUBS, 2 * step)]
        got = lax.ppermute(x, "sub", pairs)
        x = jnp.where(sub % (2 * step) == step, got, x)
    return x


def local(parent_front, child_schur, index_map):
    sub, row, col = (lax.axis_index(name) for name in ("sub", "row", "col"))
    shard = sub * ROWS + row
    where = jnp.stack([shard // (SHARDS // 2), col, row, shard]).astype(jnp.int32)
    parent = parent_front.reshape(SHARDS, BLK, WIDE)
    parent_top = from_first(parent[:TOP], sub)
    parent_rest = from_first(parent[TOP:], sub)

    low = call(
        spread_low_kernel,
        jax.ShapeDtypeStruct((SUBS, 2 * ROWS, BLK, TILE), jnp.float32),
        (where, index_map, child_schur),
        4,
    )
    low = exchange(low.reshape(SHARDS, 2, BLK, TILE), ("sub", "row"))
    tops, _ = call(
        place_top_kernel,
        (TOPS, jax.ShapeDtypeStruct((TOP, BLK, WIDE), jnp.float32)),
        (where, index_map, low, parent_top),
        6,
    )
    spread = call(
        spread_kernel,
        jax.ShapeDtypeStruct((2 * SHARDS, BLK, TILE), jnp.float32),
        (where, index_map, child_schur),
        4,
    )
    tops, spread = lax.optimization_barrier((tops, spread))
    pivots = exchange(tops, "col")
    tail = call(
        place_rest_kernel,
        jax.ShapeDtypeStruct((2 * SHARDS, BLK, WIDE), jnp.float32),
        (where, index_map, low, parent_rest, tops, pivots),
        8,
    )
    upper = over_rows(pivots[:, :2].reshape(PANEL, WIDE))
    inv0 = first_factor(where, upper)


    spread, _ = lax.optimization_barrier((spread.reshape(SHARDS, 2, BLK, TILE), pivots))
    tail = tail.reshape(2 * PANEL, WIDE)
    received, across, _ = lax.optimization_barrier(
        (exchange(spread, ("sub", "row")), swap(tail, "row", 2), inv0)
    )
    tail = tail, swap(tail, "row", 1), across, swap(across, "row", 1)
    front, tops = call(place_kernel, (FRONT, TOPS), (where, index_map, received, parent), 6)
    inv1, x01 = second_factor(where, inv0, upper, tail)
    cols = exchange(tops, "col").reshape(COLS, TOP * BLK, WIDE)
    out = finish(where, inv0, inv1, x01, cols, tail, front)
    return out.reshape(parent_front.shape)


def solution(mesh):
    spec = P(None, "col", None, ("sub", "row"))
    in_specs = (spec, P(("sub", "row", "col"), None), P())
    return jax.shard_map(local, mesh=mesh, in_specs=in_specs, out_specs=spec, check_vma=False)
```

```python
import functools

import jax
import jax.numpy as jnp
from jax import lax
from jax.experimental import pallas as pl
from jax.experimental.pallas import tpu as pltpu
from jax.sharding import PartitionSpec as P

BLK = 16
TILE = 128
STEP = 8
SUBS = 8
ROWS = 4
COLS = 16
SHARDS = SUBS * ROWS
WIDE = 256
PANEL = 512
TOP = 4

VMEM = pl.BlockSpec(memory_space=pltpu.VMEM)
SMEM = pl.BlockSpec(memory_space=pltpu.SMEM)
HBM = pl.BlockSpec(memory_space=pl.ANY)


def params(mib):
    return pltpu.CompilerParams(vmem_limit_bytes=mib << 20)


def split(a):
    high = a.astype(jnp.bfloat16)
    return high, (a - high.astype(jnp.float32)).astype(jnp.bfloat16)


def contract_split(a, b, dims):
    def product(x, y):
        return lax.dot_general(
            x, y, ((dims[:1], dims[1:]), ((), ())), preferred_element_type=jnp.float32
        )

    return product(a[0], b[1]) + product(a[1], b[0]) + product(a[0], b[0])


def spread_kernel(where_ref, map_ref, child_ref, out_ref):
    child = where_ref[0]
    out_ref[...] = jnp.zeros_like(out_ref)
    lane_block = lax.broadcasted_iota(jnp.int32, (BLK, TILE), 1) // BLK

    def body(tile, carry):
        rows = child_ref[:, pl.ds(pl.multiple_of(tile * TILE, TILE), TILE)]
        for part in range(TILE // BLK):
            block = map_ref[child, tile * (TILE // BLK) + part]
            place = block % (TILE // BLK)
            target = block // (TILE // BLK)
            shift = (place - part + TILE // BLK) % (TILE // BLK) * BLK
            moved = pltpu.roll(rows, shift, 1)
            out_ref[target] = jnp.where(lane_block == place, moved, out_ref[target])
        return carry

    lax.fori_loop(0, child_ref.shape[1] // TILE, body, 0)


def spread_low_kernel(where_ref, map_ref, child_ref, out_ref, from_ref):
    child = where_ref[0]
    part = TILE // BLK
    count = 2 * ROWS
    lane_block = lax.broadcasted_iota(jnp.int32, (BLK, TILE), 1) // BLK

    def clear(block, carry):
        from_ref[block] = -1
        return carry

    def note(block, carry):
        from_ref[map_ref[child, block]] = block
        return carry

    lax.fori_loop(0, count * part, clear, 0, unroll=8)
    lax.fori_loop(0, map_ref.shape[1], note, 0, unroll=8)
    for target in range(count):
        tile = jnp.zeros((BLK, TILE), jnp.float32)
        for place in range(part):
            block = from_ref[target * part + place]
            source = jnp.maximum(block, 0)
            rows = child_ref[:, pl.ds(pl.multiple_of(source // part * TILE, TILE), TILE)]
            moved = pltpu.roll(rows, (place - source % part + part) % part * BLK, 1)
            tile = jnp.where((lane_block == place) & (block >= 0), moved, tile)
        for sub in range(SUBS):
            out_ref[sub, target] = tile


def each_source(where_ref, map_ref, use):
    col = where_ref[1]

    def body(source, carry):
        child = source // (SHARDS // 2)
        block = map_ref[child, source % (SHARDS // 2) * COLS + col]
        use(source, block // (2 * COLS) * 2 + block % 2)
        return carry

    lax.fori_loop(0, SHARDS, body, 0)


def add_block(out_ref, slot, parent, received_ref, source):
    for half in range(2):
        lanes = slice(half * TILE, (half + 1) * TILE)
        out_ref[slot, :, lanes] = parent[:, lanes] + received_ref[source, half]


def place_kernel(where_ref, map_ref, received_ref, parent_ref, out_ref, top_ref):
    def use(source, slot):
        add_block(out_ref, slot, parent_ref[slot], received_ref, source)

    each_source(where_ref, map_ref, use)
    for q in range(COLS):
        top_ref[q] = out_ref[:TOP]


def place_top_kernel(where_ref, map_ref, received_ref, parent_ref, top_ref, out_ref):
    def use(source, slot):
        @pl.when(slot < TOP)
        def _():
            add_block(out_ref, slot, parent_ref[slot], received_ref, source)

    each_source(where_ref, map_ref, use)
    for q in range(COLS):
        top_ref[q] = out_ref[...]


def place_rest_kernel(where_ref, map_ref, received_ref, parent_ref, top_ref, pivots_ref, out_ref):
    def use(source, slot):
        @pl.when(slot >= TOP)
        def _():
            add_block(out_ref, SHARDS + slot, parent_ref[slot - TOP], received_ref, source)

    each_source(where_ref, map_ref, use)
    for q in range(COLS):
        for half in range(2):
            out_ref[2 * q + half] = pivots_ref[q, 2 + half]
    out_ref[SHARDS : SHARDS + TOP] = top_ref[0]


FRONT = jax.ShapeDtypeStruct((SHARDS, BLK, WIDE), jnp.float32)
TOPS = jax.ShapeDtypeStruct((COLS, TOP, BLK, WIDE), jnp.float32)


def call(kernel, out_shape, operands, mib, scratch=(), flops=None):
    cost = flops and pl.CostEstimate(flops=flops, bytes_accessed=4 << 20, transcendentals=0)
    return pl.pallas_call(
        kernel,
        out_shape=out_shape,
        in_specs=[SMEM, SMEM] + [VMEM] * (len(operands) - 2),
        out_specs=jax.tree.map(lambda _: VMEM, out_shape),
        scratch_shapes=list(scratch),
        compiler_params=params(mib),
        cost_estimate=cost,
        name=kernel.__name__.removesuffix("_kernel"),
    )(*operands)


def tree_sum(terms):
    while len(terms) > 1:
        terms = [sum(terms[i : i + 2]) for i in range(0, len(terms), 2)]
    return terms[0]


def factor_tile(read, out_ref):
    full = (8, TILE)
    groups = TILE // 8
    sub = lax.broadcasted_iota(jnp.int32, full, 0)
    lane = lax.broadcasted_iota(jnp.int32, full, 1)
    a = [read(h) for h in range(groups)]
    e = [jnp.where(lane == sub + 8 * h, jnp.float32(1), jnp.float32(0)) for h in range(groups)]
    for j in range(0, TILE, STEP):
        g, r = divmod(j, 8)
        col = [
            [jnp.broadcast_to(a[h][:, j + t : j + t + 1], full) for t in range(STEP)]
            for h in range(g, groups)
        ]
        p = [
            [jnp.broadcast_to(col[0][t][r + s : r + s + 1, :], full) for t in range(s + 1)]
            for s in range(STEP)
        ]
        ua = [jnp.broadcast_to(a[g][r + s : r + s + 1, :], full) for s in range(STEP)]
        ue = [jnp.broadcast_to(e[g][r + s : r + s + 1, :], full) for s in range(STEP)]
        rd = [None] * STEP
        low = [[None] * STEP for _ in range(STEP)]
        for t in range(STEP):
            rd[t] = 1.0 / p[t][t]
            for s in range(t + 1, STEP):
                low[s][t] = p[s][t] * rd[t]
            for s in range(t + 1, STEP):
                for q in range(t + 1, s + 1):
                    p[s][q] = p[s][q] - low[s][t] * p[q][t]
            for s in range(t + 1, STEP):
                ua[s] = ua[s] - low[s][t] * ua[t]
                ue[s] = ue[s] - low[s][t] * ue[t]
        for s in range(STEP):
            out_ref[j + s : j + s + 1, :] = (ue[s] * lax.rsqrt(p[s][s]))[0:1, :]
        if j + STEP >= TILE:
            break
        za = [ua[s] * rd[s] for s in range(STEP)]
        ze = [ue[s] * rd[s] for s in range(STEP)]
        for t in range(STEP - 1, 0, -1):
            for s in range(t):
                za[s] = za[s] - low[t][s] * za[t]
                ze[s] = ze[s] - low[t][s] * ze[t]
        for h in range(g, groups):
            if h == g and r + STEP >= 8:
                continue
            c = col[h - g]
            da = tree_sum([c[t] * za[t] for t in range(STEP)])
            de = tree_sum([c[t] * ze[t] for t in range(STEP)])
            if h == g:
                da = jnp.where(sub >= r + STEP, da, 0.0)
                de = jnp.where(sub >= r + STEP, de, 0.0)
            a[h] = a[h] - da
            e[h] = e[h] - de


def multiply(a, b, dims):
    return contract_split(split(a), split(b), dims)


def invert_factor(m_ref, w_ref, t_ref):
    tiles = m_ref.shape[0] // TILE
    w_ref[...] = jnp.zeros_like(w_ref)

    def body(b, carry):
        low = pl.multiple_of(b * TILE, TILE)
        factor_tile(
            lambda h: m_ref[pl.ds(pl.multiple_of(low + 8 * h, 8), 8), pl.ds(low, TILE)], t_ref
        )
        for c in range(tiles):

            @pl.when(b == c)
            def _():
                lo, hi = c * TILE, (c + 1) * TILE
                t = t_ref[...]
                if c:
                    w_ref[lo:hi, :lo] = multiply(t, w_ref[lo:hi, :lo], (1, 0))
                w_ref[lo:hi, lo:hi] = t
                if c + 1 < tiles:
                    x = multiply(t, m_ref[lo:hi, hi:], (1, 0))
                    m_ref[hi:, hi:] = m_ref[hi:, hi:] - multiply(x, x, (0, 0))
                    w_ref[hi:, :hi] = w_ref[hi:, :hi] - multiply(x, w_ref[lo:hi, :hi], (0, 0))

        return carry

    lax.fori_loop(0, tiles, body, 0)


def chunk_of(row, number):
    return (row // 2 ^ number // 2) * 2 + (row % 2 ^ number % 2)


def each_chunk(row, refs, use, first=0, last=ROWS):
    for number, ref in enumerate(refs):
        chunk = chunk_of(row, number)

        @pl.when((chunk >= first) & (chunk < last))
        def _():
            use(number, ref, pl.ds(pl.multiple_of((chunk - first) * WIDE, WIDE), WIDE))


def first_kernel(where_ref, own, core, across, both, w_ref, m_ref, t_ref, sems):
    def copy(number, ref, lanes):
        return pltpu.make_async_copy(ref, m_ref.at[:, lanes], sems.at[number])

    row, refs = where_ref[2], (own, core, across, both)
    each_chunk(row, refs, lambda *at: copy(*at).start(), 0, 2)
    each_chunk(row, refs, lambda *at: copy(*at).wait(), 0, 2)
    invert_factor(m_ref, w_ref, t_ref)


def square():
    return pltpu.VMEM((PANEL, PANEL), jnp.float32)


def first_factor(where, pieces):
    return pl.pallas_call(
        first_kernel,
        out_shape=jax.ShapeDtypeStruct((PANEL, PANEL), jnp.float32),
        in_specs=[SMEM] + [HBM] * 4,
        out_specs=VMEM,
        scratch_shapes=[
            square(),
            pltpu.VMEM((TILE, TILE), jnp.float32),
            pltpu.SemaphoreType.DMA((4,)),
        ],
        compiler_params=params(60),
        cost_estimate=pl.CostEstimate(flops=60_000_000_000, bytes_accessed=4 << 20, transcendentals=0),
        name="first_factor",
    )(where, *pieces)


def second_kernel(where_ref, inv_hbm, *refs):
    upper, lower, refs = refs[:4], refs[4:8], refs[8:]
    w_hbm, x_hbm, inv_ref, a_ref, m_ref, w_ref, x_ref, t_ref, sems = refs

    def copy_upper(number, ref, lanes):
        return pltpu.make_async_copy(ref, a_ref.at[:, lanes], sems.at[number])

    def copy_lower(number, ref, lanes):
        rows = ref.at[pl.ds(0, PANEL), :]
        return pltpu.make_async_copy(rows, m_ref.at[:, lanes], sems.at[4 + number])

    row = where_ref[2]
    inv = pltpu.make_async_copy(inv_hbm, inv_ref, sems.at[8])
    inv.start()
    each_chunk(row, upper, lambda *at: copy_upper(*at).start(), 2, 4)
    each_chunk(row, lower, lambda *at: copy_lower(*at).start(), 2, 4)
    inv.wait()
    each_chunk(row, upper, lambda *at: copy_upper(*at).wait(), 2, 4)
    x_ref[...] = multiply(inv_ref[...], a_ref[...], (1, 0))
    out = pltpu.make_async_copy(x_ref, x_hbm, sems.at[9])
    out.start()
    x = x_ref[...]
    each_chunk(row, lower, lambda *at: copy_lower(*at).wait(), 2, 4)
    m_ref[...] = m_ref[...] - multiply(x, x, (0, 0))
    invert_factor(m_ref, w_ref, t_ref)
    last = pltpu.make_async_copy(w_ref, w_hbm, sems.at[10])
    last.start()
    out.wait()
    last.wait()


def second_factor(where, inv, upper, lower):
    shape = jax.ShapeDtypeStruct((PANEL, PANEL), jnp.float32)
    return pl.pallas_call(
        second_kernel,
        out_shape=(shape, shape),
        in_specs=[SMEM] + [HBM] * 9,
        out_specs=(HBM, HBM),
        scratch_shapes=[
            square(), square(), square(), square(), square(),
            pltpu.VMEM((TILE, TILE), jnp.float32),
            pltpu.SemaphoreType.DMA((11,)),
        ],
        compiler_params=params(60),
        cost_estimate=pl.CostEstimate(flops=60_000_000_000, bytes_accessed=8 << 20, transcendentals=0),
        name="second_factor",
    )(where, inv, *upper, *lower)


def finish_kernel(
    where_ref, inv0_hbm, inv1_hbm, x01_hbm, cols_hbm, row0, row1, row2, row3, front_hbm, out_ref,
    inv0_ref, inv1_ref, x01_ref, rows_ref, cols0_ref, cols1_ref, front_ref, sems,
):
    col, row, shard = where_ref[1], where_ref[2], where_ref[3]
    refs = (row0, row1, row2, row3)

    def copy_rows(number, ref, lanes):
        return pltpu.make_async_copy(
            ref.at[pl.ds(PANEL, PANEL), :], rows_ref.at[:, lanes], sems.at[number]
        )

    copies = [
        (inv0_hbm, inv0_ref),
        (cols_hbm.at[:, pl.ds(0, 2 * BLK), :], cols0_ref),
        (cols_hbm.at[:, pl.ds(2 * BLK, 2 * BLK), :], cols1_ref),
        (x01_hbm, x01_ref),
        (inv1_hbm, inv1_ref),
        (front_hbm, front_ref),
    ]
    copies = [
        pltpu.make_async_copy(source, target, sems.at[4 + i])
        for i, (source, target) in enumerate(copies)
    ]
    each_chunk(row, refs, lambda *at: copy_rows(*at).start())
    for copy in copies:
        copy.start()
    each_chunk(row, refs, lambda *at: copy_rows(*at).wait())
    for copy in copies:
        copy.wait()
    inv0, inv1, x01 = split(inv0_ref[...]), split(inv1_ref[...]), split(x01_ref[...])
    r0 = split(contract_split(split(rows_ref[:, :PANEL]), inv0, (1, 1)))
    c0 = contract_split(inv0, split(cols0_ref[...].reshape(PANEL, WIDE)), (1, 0))
    cols0_ref[...] = c0.reshape(cols0_ref.shape)
    c0 = split(c0)
    r1 = split(rows_ref[:, PANEL:] - contract_split(r0, x01, (1, 0)))
    r1 = split(contract_split(r1, inv1, (1, 1)))
    c1 = split(cols1_ref[...].reshape(PANEL, WIDE) - contract_split(x01, c0, (0, 0)))
    c1 = contract_split(inv1, c1, (1, 0))
    cols1_ref[...] = c1.reshape(cols1_ref.shape)
    update = contract_split(r0, c0, (1, 0)) + contract_split(r1, split(c1), (1, 0))
    live = (shard >= ROWS).astype(jnp.float32)
    for slot in range(TOP, SHARDS):
        rows = slice(slot * BLK, (slot + 1) * BLK)
        out_ref[slot] = (front_ref[slot] - update[rows]) * live
    past = (shard >= ROWS // 2).astype(jnp.float32)
    for half in range(2):
        rows = slice(half * BLK, (half + 1) * BLK)
        out_ref[half] = cols0_ref[col, rows, :]
        out_ref[2 + half] = cols1_ref[col, rows, :] * past


def finish(where, inv0, inv1, x01, cols, rows, front):
    return pl.pallas_call(
        finish_kernel,
        out_shape=FRONT,
        in_specs=[SMEM] + [HBM] * 9,
        out_specs=VMEM,
        scratch_shapes=[
            square(), square(), square(),
            pltpu.VMEM((PANEL, 2 * PANEL), jnp.float32),
            pltpu.VMEM((COLS, 2 * BLK, WIDE), jnp.float32),
            pltpu.VMEM((COLS, 2 * BLK, WIDE), jnp.float32),
            pltpu.VMEM((SHARDS, BLK, WIDE), jnp.float32),
            pltpu.SemaphoreType.DMA((10,)),
        ],
        compiler_params=params(60),
        name="finish",
    )(where, inv0, inv1, x01, cols, *rows, front)


def swap(x, axis, bit):
    return lax.ppermute(x, axis, [(i, i ^ bit) for i in range(ROWS)])


def to_all(x, axis, count):
    return lax.all_to_all(
        jnp.broadcast_to(x[None], (count, *x.shape)), axis, split_axis=0, concat_axis=0, tiled=True
    )


def exchange(x, axis):
    return lax.all_to_all(x, axis, split_axis=0, concat_axis=0, tiled=True)


def over_rows(x):
    across = swap(x, "row", 2)
    return x, swap(x, "row", 1), across, swap(across, "row", 1)


def from_first(x, sub, beside=None):
    for step in (4, 2, 1):
        pairs = [(i, i + step) for i in range(0, SUBS, 2 * step)]
        got = lax.ppermute(x, "sub", pairs)
        if beside is not None and step == 4:
            got, _ = lax.optimization_barrier((got, beside))
        x = jnp.where(sub % (2 * step) == step, got, x)
    return x


def local(parent_front, child_schur, index_map):
    sub, row, col = (lax.axis_index(name) for name in ("sub", "row", "col"))
    shard = sub * ROWS + row
    where = jnp.stack([shard // (SHARDS // 2), col, row, shard]).astype(jnp.int32)
    parent = parent_front.reshape(SHARDS, BLK, WIDE)
    parent_top = from_first(parent[:TOP], sub)

    low = call(
        spread_low_kernel,
        jax.ShapeDtypeStruct((SUBS, 2 * ROWS, BLK, TILE), jnp.float32),
        (where, index_map, child_schur),
        4,
        [pltpu.SMEM((2 * SHARDS * TILE // BLK,), jnp.int32)],
    )
    low = exchange(low.reshape(SHARDS, 2, BLK, TILE), ("sub", "row"))
    tops, _ = call(
        place_top_kernel,
        (TOPS, jax.ShapeDtypeStruct((TOP, BLK, WIDE), jnp.float32)),
        (where, index_map, low, parent_top),
        6,
    )
    tops, child_late = lax.optimization_barrier((tops, child_schur))
    pivots = exchange(tops, "col")
    spread = call(
        spread_kernel,
        jax.ShapeDtypeStruct((2 * SHARDS, BLK, TILE), jnp.float32),
        (where, index_map, child_late),
        4,
    )
    parent_rest = from_first(parent[TOP:], sub, spread)
    tail = call(
        place_rest_kernel,
        jax.ShapeDtypeStruct((2 * SHARDS, BLK, WIDE), jnp.float32),
        (where, index_map, low, parent_rest, tops, pivots),
        8,
    )
    upper = over_rows(pivots[:, :2].reshape(PANEL, WIDE))
    inv0 = first_factor(where, upper)


    spread, _ = lax.optimization_barrier((spread.reshape(SHARDS, 2, BLK, TILE), pivots))
    tail = tail.reshape(2 * PANEL, WIDE)
    received, across, _ = lax.optimization_barrier(
        (exchange(spread, ("sub", "row")), swap(tail, "row", 2), inv0)
    )
    tail = tail, swap(tail, "row", 1), across, swap(across, "row", 1)
    front, tops = call(place_kernel, (FRONT, TOPS), (where, index_map, received, parent), 6)
    inv1, x01 = second_factor(where, inv0, upper, tail)
    cols = exchange(tops, "col").reshape(COLS, TOP * BLK, WIDE)
    out = finish(where, inv0, inv1, x01, cols, tail, front)
    return out.reshape(parent_front.shape)


def solution(mesh):
    spec = P(None, "col", None, ("sub", "row"))
    in_specs = (spec, P(("sub", "row", "col"), None), P())
    return jax.shard_map(local, mesh=mesh, in_specs=in_specs, out_specs=spec, check_vma=False)
```

```python
import functools

import jax
import jax.numpy as jnp
from jax import lax
from jax.experimental import pallas as pl
from jax.experimental.pallas import tpu as pltpu
from jax.sharding import PartitionSpec as P

BLK = 16
TILE = 128
STEP = 8
SUBS = 8
ROWS = 4
COLS = 16
SHARDS = SUBS * ROWS
WIDE = 256
PANEL = 512
TOP = 4

VMEM = pl.BlockSpec(memory_space=pltpu.VMEM)
SMEM = pl.BlockSpec(memory_space=pltpu.SMEM)
HBM = pl.BlockSpec(memory_space=pl.ANY)


def params(mib):
    return pltpu.CompilerParams(vmem_limit_bytes=mib << 20)


def split(a):
    high = a.astype(jnp.bfloat16)
    return high, (a - high.astype(jnp.float32)).astype(jnp.bfloat16)


def contract_split(a, b, dims):
    def product(x, y):
        return lax.dot_general(
            x, y, ((dims[:1], dims[1:]), ((), ())), preferred_element_type=jnp.float32
        )

    return product(a[0], b[1]) + product(a[1], b[0]) + product(a[0], b[0])


def spread_kernel(where_ref, map_ref, child_ref, out_ref):
    child = where_ref[0]
    out_ref[...] = jnp.zeros_like(out_ref)
    lane_block = lax.broadcasted_iota(jnp.int32, (BLK, TILE), 1) // BLK

    def body(tile, carry):
        rows = child_ref[:, pl.ds(pl.multiple_of(tile * TILE, TILE), TILE)]
        for part in range(TILE // BLK):
            block = map_ref[child, tile * (TILE // BLK) + part]
            place = block % (TILE // BLK)
            target = block // (TILE // BLK)
            shift = (place - part + TILE // BLK) % (TILE // BLK) * BLK
            moved = pltpu.roll(rows, shift, 1)
            out_ref[target] = jnp.where(lane_block == place, moved, out_ref[target])
        return carry

    lax.fori_loop(0, child_ref.shape[1] // TILE, body, 0)


def spread_low_kernel(where_ref, map_ref, child_ref, out_ref, from_ref):
    child = where_ref[0]
    part = TILE // BLK
    count = 2 * ROWS
    lane_block = lax.broadcasted_iota(jnp.int32, (BLK, TILE), 1) // BLK

    def clear(block, carry):
        from_ref[block] = -1
        return carry

    def note(block, carry):
        from_ref[map_ref[child, block]] = block
        return carry

    lax.fori_loop(0, count * part, clear, 0, unroll=8)
    lax.fori_loop(0, map_ref.shape[1], note, 0, unroll=8)
    for target in range(count):
        tile = jnp.zeros((BLK, TILE), jnp.float32)
        for place in range(part):
            block = from_ref[target * part + place]
            source = jnp.maximum(block, 0)
            rows = child_ref[:, pl.ds(pl.multiple_of(source // part * TILE, TILE), TILE)]
            moved = pltpu.roll(rows, (place - source % part + part) % part * BLK, 1)
            tile = jnp.where((lane_block == place) & (block >= 0), moved, tile)
        for sub in range(SUBS):
            out_ref[sub, target] = tile


def find_sources(where_ref, map_ref, from_ref):
    col = where_ref[1]
    for source in range(SHARDS):
        child, number = divmod(source, SHARDS // 2)
        block = map_ref[child, number * COLS + col]
        from_ref[block // (2 * COLS) * 2 + block % 2] = source


def add_block(out_ref, at, parent, received_ref, source):
    for half in range(2):
        lanes = slice(half * TILE, (half + 1) * TILE)
        out_ref[at, :, lanes] = parent[:, lanes] + received_ref[source, half]


def place_kernel(where_ref, map_ref, received_ref, parent_ref, out_ref, top_ref, from_ref):
    find_sources(where_ref, map_ref, from_ref)
    for slot in range(SHARDS):
        add_block(out_ref, slot, parent_ref[slot], received_ref, from_ref[slot])
    for q in range(COLS):
        top_ref[q] = out_ref[:TOP]


def place_top_kernel(where_ref, map_ref, received_ref, parent_ref, top_ref, from_ref):
    find_sources(where_ref, map_ref, from_ref)
    for slot in range(TOP):
        for half in range(2):
            lanes = slice(half * TILE, (half + 1) * TILE)
            block = parent_ref[slot, :, lanes] + received_ref[from_ref[slot], half]
            for q in range(COLS):
                top_ref[q, slot, :, lanes] = block


def place_rest_kernel(
    where_ref, map_ref, received_ref, parent_ref, top_ref, pivots_ref, out_ref, from_ref
):
    find_sources(where_ref, map_ref, from_ref)
    for slot in range(TOP, SHARDS):
        add_block(out_ref, SHARDS + slot, parent_ref[slot - TOP], received_ref, from_ref[slot])
    for q in range(COLS):
        for half in range(2):
            out_ref[2 * q + half] = pivots_ref[q, 2 + half]
    out_ref[SHARDS : SHARDS + TOP] = top_ref[0]


SOURCES = [pltpu.SMEM((SHARDS,), jnp.int32)]
FRONT = jax.ShapeDtypeStruct((SHARDS, BLK, WIDE), jnp.float32)
TOPS = jax.ShapeDtypeStruct((COLS, TOP, BLK, WIDE), jnp.float32)


def call(kernel, out_shape, operands, mib, scratch=(), flops=None):
    cost = flops and pl.CostEstimate(flops=flops, bytes_accessed=4 << 20, transcendentals=0)
    return pl.pallas_call(
        kernel,
        out_shape=out_shape,
        in_specs=[SMEM, SMEM] + [VMEM] * (len(operands) - 2),
        out_specs=jax.tree.map(lambda _: VMEM, out_shape),
        scratch_shapes=list(scratch),
        compiler_params=params(mib),
        cost_estimate=cost,
        name=kernel.__name__.removesuffix("_kernel"),
    )(*operands)


def tree_sum(terms):
    while len(terms) > 1:
        terms = [sum(terms[i : i + 2]) for i in range(0, len(terms), 2)]
    return terms[0]


def factor_tile(read, out_ref):
    full = (8, TILE)
    groups = TILE // 8
    sub = lax.broadcasted_iota(jnp.int32, full, 0)
    lane = lax.broadcasted_iota(jnp.int32, full, 1)
    a = [read(h) for h in range(groups)]
    e = [jnp.where(lane == sub + 8 * h, jnp.float32(1), jnp.float32(0)) for h in range(groups)]
    for j in range(0, TILE, STEP):
        g, r = divmod(j, 8)
        col = [
            [jnp.broadcast_to(a[h][:, j + t : j + t + 1], full) for t in range(STEP)]
            for h in range(g, groups)
        ]
        p = [
            [jnp.broadcast_to(col[0][t][r + s : r + s + 1, :], full) for t in range(s + 1)]
            for s in range(STEP)
        ]
        ua = [jnp.broadcast_to(a[g][r + s : r + s + 1, :], full) for s in range(STEP)]
        ue = [jnp.broadcast_to(e[g][r + s : r + s + 1, :], full) for s in range(STEP)]
        rd = [None] * STEP
        low = [[None] * STEP for _ in range(STEP)]
        for t in range(STEP):
            rd[t] = 1.0 / p[t][t]
            for s in range(t + 1, STEP):
                low[s][t] = p[s][t] * rd[t]
            for s in range(t + 1, STEP):
                for q in range(t + 1, s + 1):
                    p[s][q] = p[s][q] - low[s][t] * p[q][t]
            for s in range(t + 1, STEP):
                ua[s] = ua[s] - low[s][t] * ua[t]
                ue[s] = ue[s] - low[s][t] * ue[t]
        for s in range(STEP):
            out_ref[j + s : j + s + 1, :] = (ue[s] * lax.rsqrt(p[s][s]))[0:1, :]
        if j + STEP >= TILE:
            break
        za = [ua[s] * rd[s] for s in range(STEP)]
        ze = [ue[s] * rd[s] for s in range(STEP)]
        for t in range(STEP - 1, 0, -1):
            for s in range(t):
                za[s] = za[s] - low[t][s] * za[t]
                ze[s] = ze[s] - low[t][s] * ze[t]
        for h in range(g, groups):
            if h == g and r + STEP >= 8:
                continue
            c = col[h - g]
            da = tree_sum([c[t] * za[t] for t in range(STEP)])
            de = tree_sum([c[t] * ze[t] for t in range(STEP)])
            if h == g:
                da = jnp.where(sub >= r + STEP, da, 0.0)
                de = jnp.where(sub >= r + STEP, de, 0.0)
            a[h] = a[h] - da
            e[h] = e[h] - de


def multiply(a, b, dims):
    return contract_split(split(a), split(b), dims)


def invert_factor(m_ref, w_ref, t_ref):
    tiles = m_ref.shape[0] // TILE
    w_ref[...] = jnp.zeros_like(w_ref)

    def body(b, carry):
        low = pl.multiple_of(b * TILE, TILE)
        factor_tile(
            lambda h: m_ref[pl.ds(pl.multiple_of(low + 8 * h, 8), 8), pl.ds(low, TILE)], t_ref
        )
        for c in range(tiles):

            @pl.when(b == c)
            def _():
                lo, hi = c * TILE, (c + 1) * TILE
                t = t_ref[...]
                if c:
                    w_ref[lo:hi, :lo] = multiply(t, w_ref[lo:hi, :lo], (1, 0))
                w_ref[lo:hi, lo:hi] = t
                if c + 1 < tiles:
                    x = multiply(t, m_ref[lo:hi, hi:], (1, 0))
                    m_ref[hi:, hi:] = m_ref[hi:, hi:] - multiply(x, x, (0, 0))
                    w_ref[hi:, :hi] = w_ref[hi:, :hi] - multiply(x, w_ref[lo:hi, :hi], (0, 0))

        return carry

    lax.fori_loop(0, tiles, body, 0)


def chunk_of(row, number):
    return (row // 2 ^ number // 2) * 2 + (row % 2 ^ number % 2)


def each_chunk(row, refs, use, first=0, last=ROWS):
    for number, ref in enumerate(refs):
        chunk = chunk_of(row, number)

        @pl.when((chunk >= first) & (chunk < last))
        def _():
            use(number, ref, pl.ds(pl.multiple_of((chunk - first) * WIDE, WIDE), WIDE))


def first_kernel(where_ref, own, core, across, both, w_ref, m_ref, t_ref, sems):
    def copy(number, ref, lanes):
        return pltpu.make_async_copy(ref, m_ref.at[:, lanes], sems.at[number])

    row, refs = where_ref[2], (own, core, across, both)
    each_chunk(row, refs, lambda *at: copy(*at).start(), 0, 2)
    each_chunk(row, refs, lambda *at: copy(*at).wait(), 0, 2)
    invert_factor(m_ref, w_ref, t_ref)


def square():
    return pltpu.VMEM((PANEL, PANEL), jnp.float32)


def first_factor(where, pieces):
    return pl.pallas_call(
        first_kernel,
        out_shape=jax.ShapeDtypeStruct((PANEL, PANEL), jnp.float32),
        in_specs=[SMEM] + [HBM] * 4,
        out_specs=VMEM,
        scratch_shapes=[
            square(),
            pltpu.VMEM((TILE, TILE), jnp.float32),
            pltpu.SemaphoreType.DMA((4,)),
        ],
        compiler_params=params(60),
        cost_estimate=pl.CostEstimate(flops=60_000_000_000, bytes_accessed=4 << 20, transcendentals=0),
        name="first_factor",
    )(where, *pieces)


def second_kernel(where_ref, inv_hbm, *refs):
    upper, lower, refs = refs[:4], refs[4:8], refs[8:]
    w_hbm, x_hbm, inv_ref, a_ref, m_ref, w_ref, x_ref, t_ref, sems = refs

    def copy_upper(number, ref, lanes):
        return pltpu.make_async_copy(ref, a_ref.at[:, lanes], sems.at[number])

    def copy_lower(number, ref, lanes):
        rows = ref.at[pl.ds(0, PANEL), :]
        return pltpu.make_async_copy(rows, m_ref.at[:, lanes], sems.at[4 + number])

    row = where_ref[2]
    inv = pltpu.make_async_copy(inv_hbm, inv_ref, sems.at[8])
    inv.start()
    each_chunk(row, upper, lambda *at: copy_upper(*at).start(), 2, 4)
    each_chunk(row, lower, lambda *at: copy_lower(*at).start(), 2, 4)
    inv.wait()
    each_chunk(row, upper, lambda *at: copy_upper(*at).wait(), 2, 4)
    x_ref[...] = multiply(inv_ref[...], a_ref[...], (1, 0))
    out = pltpu.make_async_copy(x_ref, x_hbm, sems.at[9])
    out.start()
    x = x_ref[...]
    each_chunk(row, lower, lambda *at: copy_lower(*at).wait(), 2, 4)
    m_ref[...] = m_ref[...] - multiply(x, x, (0, 0))
    invert_factor(m_ref, w_ref, t_ref)
    last = pltpu.make_async_copy(w_ref, w_hbm, sems.at[10])
    last.start()
    out.wait()
    last.wait()


def second_factor(where, inv, upper, lower):
    shape = jax.ShapeDtypeStruct((PANEL, PANEL), jnp.float32)
    return pl.pallas_call(
        second_kernel,
        out_shape=(shape, shape),
        in_specs=[SMEM] + [HBM] * 9,
        out_specs=(HBM, HBM),
        scratch_shapes=[
            square(), square(), square(), square(), square(),
            pltpu.VMEM((TILE, TILE), jnp.float32),
            pltpu.SemaphoreType.DMA((11,)),
        ],
        compiler_params=params(60),
        cost_estimate=pl.CostEstimate(flops=60_000_000_000, bytes_accessed=8 << 20, transcendentals=0),
        name="second_factor",
    )(where, inv, *upper, *lower)


def finish_kernel(
    where_ref, inv0_hbm, inv1_hbm, x01_hbm, cols_hbm, row0, row1, row2, row3, front_hbm, out_ref,
    inv0_ref, inv1_ref, x01_ref, rows_ref, cols0_ref, cols1_ref, front_ref, sems,
):
    col, row, shard = where_ref[1], where_ref[2], where_ref[3]
    refs = (row0, row1, row2, row3)

    def copy_rows(number, ref, lanes):
        return pltpu.make_async_copy(
            ref.at[pl.ds(PANEL, PANEL), :], rows_ref.at[:, lanes], sems.at[number]
        )

    copies = [
        (inv0_hbm, inv0_ref),
        (cols_hbm.at[:, pl.ds(0, 2 * BLK), :], cols0_ref),
        (cols_hbm.at[:, pl.ds(2 * BLK, 2 * BLK), :], cols1_ref),
        (x01_hbm, x01_ref),
        (inv1_hbm, inv1_ref),
        (front_hbm, front_ref),
    ]
    copies = [
        pltpu.make_async_copy(source, target, sems.at[4 + i])
        for i, (source, target) in enumerate(copies)
    ]
    for copy in copies:
        copy.start()
    each_chunk(row, refs, lambda *at: copy_rows(*at).start())
    inv0_copy, cols0_copy, cols1_copy, x01_copy, inv1_copy, front_copy = copies
    inv0_copy.wait()
    cols0_copy.wait()
    inv0 = split(inv0_ref[...])
    c0 = contract_split(inv0, split(cols0_ref[...].reshape(PANEL, WIDE)), (1, 0))
    cols0_ref[...] = c0.reshape(cols0_ref.shape)
    c0 = split(c0)
    cols1_copy.wait()
    x01_copy.wait()
    x01 = split(x01_ref[...])
    c1 = split(cols1_ref[...].reshape(PANEL, WIDE) - contract_split(x01, c0, (0, 0)))
    inv1_copy.wait()
    inv1 = split(inv1_ref[...])
    c1 = contract_split(inv1, c1, (1, 0))
    cols1_ref[...] = c1.reshape(cols1_ref.shape)
    each_chunk(row, refs, lambda *at: copy_rows(*at).wait())
    r0 = split(contract_split(split(rows_ref[:, :PANEL]), inv0, (1, 1)))
    r1 = split(rows_ref[:, PANEL:] - contract_split(r0, x01, (1, 0)))
    r1 = split(contract_split(r1, inv1, (1, 1)))
    front_copy.wait()
    update = contract_split(r0, c0, (1, 0)) + contract_split(r1, split(c1), (1, 0))
    live = (shard >= ROWS).astype(jnp.float32)
    for slot in range(TOP, SHARDS):
        rows = slice(slot * BLK, (slot + 1) * BLK)
        out_ref[slot] = (front_ref[slot] - update[rows]) * live
    past = (shard >= ROWS // 2).astype(jnp.float32)
    for half in range(2):
        rows = slice(half * BLK, (half + 1) * BLK)
        out_ref[half] = cols0_ref[col, rows, :]
        out_ref[2 + half] = cols1_ref[col, rows, :] * past


def finish(where, inv0, inv1, x01, cols, rows, front):
    return pl.pallas_call(
        finish_kernel,
        out_shape=FRONT,
        in_specs=[SMEM] + [HBM] * 9,
        out_specs=VMEM,
        scratch_shapes=[
            square(), square(), square(),
            pltpu.VMEM((PANEL, 2 * PANEL), jnp.float32),
            pltpu.VMEM((COLS, 2 * BLK, WIDE), jnp.float32),
            pltpu.VMEM((COLS, 2 * BLK, WIDE), jnp.float32),
            pltpu.VMEM((SHARDS, BLK, WIDE), jnp.float32),
            pltpu.SemaphoreType.DMA((10,)),
        ],
        compiler_params=params(59),
        name="finish",
    )(where, inv0, inv1, x01, cols, *rows, front)


def swap(x, axis, bit):
    return lax.ppermute(x, axis, [(i, i ^ bit) for i in range(ROWS)])


def to_all(x, axis, count):
    return lax.all_to_all(
        jnp.broadcast_to(x[None], (count, *x.shape)), axis, split_axis=0, concat_axis=0, tiled=True
    )


def exchange(x, axis):
    return lax.all_to_all(x, axis, split_axis=0, concat_axis=0, tiled=True)


def over_rows(x):
    across = swap(x, "row", 2)
    return x, swap(x, "row", 1), across, swap(across, "row", 1)


def from_first(x, sub, beside=None):
    for step in (4, 2, 1):
        pairs = [(i, i + step) for i in range(0, SUBS, 2 * step)]
        got = lax.ppermute(x, "sub", pairs)
        if step == 4:
            got, beside = lax.optimization_barrier((got, beside))
        x = jnp.where(sub % (2 * step) == step, got, x)
    return x, beside


def local(parent_front, child_schur, index_map):
    sub, row, col = (lax.axis_index(name) for name in ("sub", "row", "col"))
    shard = sub * ROWS + row
    where = jnp.stack([shard // (SHARDS // 2), col, row, shard]).astype(jnp.int32)
    parent = parent_front.reshape(SHARDS, BLK, WIDE)

    low = call(
        spread_low_kernel,
        jax.ShapeDtypeStruct((SUBS, 2 * ROWS, BLK, TILE), jnp.float32),
        (where, index_map, child_schur),
        4,
        [pltpu.SMEM((2 * SHARDS * TILE // BLK,), jnp.int32)],
    )
    parent_top, low = from_first(parent[:TOP], sub, low)
    low = exchange(low.reshape(SHARDS, 2, BLK, TILE), ("sub", "row"))
    tops = call(place_top_kernel, TOPS, (where, index_map, low, parent_top), 6, SOURCES)
    tops, child_late = lax.optimization_barrier((tops, child_schur))
    pivots = exchange(tops, "col")
    spread = call(
        spread_kernel,
        jax.ShapeDtypeStruct((2 * SHARDS, BLK, TILE), jnp.float32),
        (where, index_map, child_late),
        4,
    )
    parent_rest, spread = from_first(parent[TOP:], sub, spread)
    tail = call(
        place_rest_kernel,
        jax.ShapeDtypeStruct((2 * SHARDS, BLK, WIDE), jnp.float32),
        (where, index_map, low, parent_rest, tops, pivots),
        8,
        SOURCES,
    )
    upper = over_rows(pivots[:, :2].reshape(PANEL, WIDE))
    inv0 = first_factor(where, upper)


    spread, _ = lax.optimization_barrier((spread.reshape(SHARDS, 2, BLK, TILE), pivots))
    tail = tail.reshape(2 * PANEL, WIDE)
    received, across, _ = lax.optimization_barrier(
        (exchange(spread, ("sub", "row")), swap(tail, "row", 2), inv0)
    )
    tail = tail, swap(tail, "row", 1), across, swap(across, "row", 1)
    front, tops = call(place_kernel, (FRONT, TOPS), (where, index_map, received, parent), 6, SOURCES)
    inv1, x01 = second_factor(where, inv0, upper, tail)
    cols = exchange(tops, "col").reshape(COLS, TOP * BLK, WIDE)
    out = finish(where, inv0, inv1, x01, cols, tail, front)
    return out.reshape(parent_front.shape)


def solution(mesh):
    spec = P(None, "col", None, ("sub", "row"))
    in_specs = (spec, P(("sub", "row", "col"), None), P())
    return jax.shard_map(local, mesh=mesh, in_specs=in_specs, out_specs=spec, check_vma=False)
```

```python
import functools

import jax
import jax.numpy as jnp
from jax import lax
from jax.experimental import pallas as pl
from jax.experimental.pallas import tpu as pltpu
from jax.sharding import PartitionSpec as P

BLK = 16
TILE = 128
STEP = 8
SUBS = 8
ROWS = 4
COLS = 16
SHARDS = SUBS * ROWS
WIDE = 256
PANEL = 512
TOP = 4

VMEM = pl.BlockSpec(memory_space=pltpu.VMEM)
SMEM = pl.BlockSpec(memory_space=pltpu.SMEM)
HBM = pl.BlockSpec(memory_space=pl.ANY)


def params(mib):
    return pltpu.CompilerParams(vmem_limit_bytes=mib << 20)


def split(a):
    high = a.astype(jnp.bfloat16)
    return high, (a - high.astype(jnp.float32)).astype(jnp.bfloat16)


def contract_split(a, b, dims):
    def product(x, y):
        return lax.dot_general(
            x, y, ((dims[:1], dims[1:]), ((), ())), preferred_element_type=jnp.float32
        )

    return product(a[0], b[1]) + product(a[1], b[0]) + product(a[0], b[0])


def spread_kernel(where_ref, map_ref, child_ref, out_ref):
    child = where_ref[0]
    out_ref[...] = jnp.zeros_like(out_ref)
    lane_block = lax.broadcasted_iota(jnp.int32, (BLK, TILE), 1) // BLK

    def body(tile, carry):
        rows = child_ref[:, pl.ds(pl.multiple_of(tile * TILE, TILE), TILE)]
        for part in range(TILE // BLK):
            block = map_ref[child, tile * (TILE // BLK) + part]
            place = block % (TILE // BLK)
            target = block // (TILE // BLK)
            shift = (place - part + TILE // BLK) % (TILE // BLK) * BLK
            moved = pltpu.roll(rows, shift, 1)
            out_ref[target] = jnp.where(lane_block == place, moved, out_ref[target])
        return carry

    lax.fori_loop(0, child_ref.shape[1] // TILE, body, 0)


def spread_low_kernel(where_ref, map_ref, child_ref, out_ref, from_ref):
    child = where_ref[0]
    part = TILE // BLK
    count = 2 * ROWS
    lane_block = lax.broadcasted_iota(jnp.int32, (BLK, TILE), 1) // BLK

    def clear(block, carry):
        from_ref[block] = -1
        return carry

    def note(block, carry):
        from_ref[map_ref[child, block]] = block
        return carry

    lax.fori_loop(0, count * part, clear, 0, unroll=8)
    lax.fori_loop(0, map_ref.shape[1], note, 0, unroll=8)
    for target in range(count):
        tile = jnp.zeros((BLK, TILE), jnp.float32)
        for place in range(part):
            block = from_ref[target * part + place]
            source = jnp.maximum(block, 0)
            rows = child_ref[:, pl.ds(pl.multiple_of(source // part * TILE, TILE), TILE)]
            moved = pltpu.roll(rows, (place - source % part + part) % part * BLK, 1)
            tile = jnp.where((lane_block == place) & (block >= 0), moved, tile)
        for sub in range(SUBS):
            out_ref[sub, target] = tile


def find_sources(where_ref, map_ref, from_ref):
    col = where_ref[1]
    for source in range(SHARDS):
        child, number = divmod(source, SHARDS // 2)
        block = map_ref[child, number * COLS + col]
        from_ref[block // (2 * COLS) * 2 + block % 2] = source


def add_block(out_ref, at, parent, received_ref, source):
    for half in range(2):
        lanes = slice(half * TILE, (half + 1) * TILE)
        out_ref[at, :, lanes] = parent[:, lanes] + received_ref[source, half]


def place_kernel(where_ref, map_ref, received_ref, parent_ref, out_ref, top_ref, from_ref):
    find_sources(where_ref, map_ref, from_ref)
    for slot in range(SHARDS):
        add_block(out_ref, slot, parent_ref[slot], received_ref, from_ref[slot])
    for q in range(COLS):
        top_ref[q] = out_ref[:TOP]


def place_top_kernel(where_ref, map_ref, received_ref, parent_ref, top_ref, from_ref):
    find_sources(where_ref, map_ref, from_ref)
    for slot in range(TOP):
        for half in range(2):
            lanes = slice(half * TILE, (half + 1) * TILE)
            block = parent_ref[slot, :, lanes] + received_ref[from_ref[slot], half]
            for q in range(COLS):
                top_ref[q, slot, :, lanes] = block


def place_rest_kernel(
    where_ref, map_ref, received_ref, parent_ref, top_ref, pivots_ref, out_ref, from_ref
):
    find_sources(where_ref, map_ref, from_ref)
    for slot in range(TOP, SHARDS):
        add_block(out_ref, SHARDS + slot, parent_ref[slot - TOP], received_ref, from_ref[slot])
    for q in range(COLS):
        for half in range(2):
            out_ref[2 * q + half] = pivots_ref[q, 2 + half]
    out_ref[SHARDS : SHARDS + TOP] = top_ref[0]


SOURCES = [pltpu.SMEM((SHARDS,), jnp.int32)]
FRONT = jax.ShapeDtypeStruct((SHARDS, BLK, WIDE), jnp.float32)
TOPS = jax.ShapeDtypeStruct((COLS, TOP, BLK, WIDE), jnp.float32)


def call(kernel, out_shape, operands, mib, scratch=(), flops=None):
    cost = flops and pl.CostEstimate(flops=flops, bytes_accessed=4 << 20, transcendentals=0)
    return pl.pallas_call(
        kernel,
        out_shape=out_shape,
        in_specs=[SMEM, SMEM] + [VMEM] * (len(operands) - 2),
        out_specs=jax.tree.map(lambda _: VMEM, out_shape),
        scratch_shapes=list(scratch),
        compiler_params=params(mib),
        cost_estimate=cost,
        name=kernel.__name__.removesuffix("_kernel"),
    )(*operands)


def tree_sum(terms):
    while len(terms) > 1:
        terms = [sum(terms[i : i + 2]) for i in range(0, len(terms), 2)]
    return terms[0]


def factor_tile(read, out_ref):
    full = (8, TILE)
    groups = TILE // 8
    sub = lax.broadcasted_iota(jnp.int32, full, 0)
    lane = lax.broadcasted_iota(jnp.int32, full, 1)
    a = [read(h) for h in range(groups)]
    e = [jnp.where(lane == sub + 8 * h, jnp.float32(1), jnp.float32(0)) for h in range(groups)]
    for j in range(0, TILE, STEP):
        g, r = divmod(j, 8)
        col = [
            [jnp.broadcast_to(a[h][:, j + t : j + t + 1], full) for t in range(STEP)]
            for h in range(g, groups)
        ]
        p = [
            [jnp.broadcast_to(col[0][t][r + s : r + s + 1, :], full) for t in range(s + 1)]
            for s in range(STEP)
        ]
        ua = [jnp.broadcast_to(a[g][r + s : r + s + 1, :], full) for s in range(STEP)]
        ue = [jnp.broadcast_to(e[g][r + s : r + s + 1, :], full) for s in range(STEP)]
        rd = [None] * STEP
        low = [[None] * STEP for _ in range(STEP)]
        for t in range(STEP):
            rd[t] = 1.0 / p[t][t]
            for s in range(t + 1, STEP):
                low[s][t] = p[s][t] * rd[t]
            for s in range(t + 1, STEP):
                for q in range(t + 1, s + 1):
                    p[s][q] = p[s][q] - low[s][t] * p[q][t]
            for s in range(t + 1, STEP):
                ua[s] = ua[s] - low[s][t] * ua[t]
                ue[s] = ue[s] - low[s][t] * ue[t]
        for s in range(STEP):
            out_ref[j + s : j + s + 1, :] = (ue[s] * lax.rsqrt(p[s][s]))[0:1, :]
        if j + STEP >= TILE:
            break
        za = [ua[s] * rd[s] for s in range(STEP)]
        ze = [ue[s] * rd[s] for s in range(STEP)]
        for t in range(STEP - 1, 0, -1):
            for s in range(t):
                za[s] = za[s] - low[t][s] * za[t]
                ze[s] = ze[s] - low[t][s] * ze[t]
        for h in range(g, groups):
            if h == g and r + STEP >= 8:
                continue
            c = col[h - g]
            da = tree_sum([c[t] * za[t] for t in range(STEP)])
            de = tree_sum([c[t] * ze[t] for t in range(STEP)])
            if h == g:
                da = jnp.where(sub >= r + STEP, da, 0.0)
                de = jnp.where(sub >= r + STEP, de, 0.0)
            a[h] = a[h] - da
            e[h] = e[h] - de


def multiply(a, b, dims):
    return contract_split(split(a), split(b), dims)


def invert_factor(m_ref, w_ref, t_ref, beside=None):
    tiles = m_ref.shape[0] // TILE
    w_ref[...] = jnp.zeros_like(w_ref)

    def body(b, carry):
        low = pl.multiple_of(b * TILE, TILE)
        factor_tile(
            lambda h: m_ref[pl.ds(pl.multiple_of(low + 8 * h, 8), 8), pl.ds(low, TILE)], t_ref
        )
        if beside is not None:
            beside(b)
        for c in range(tiles):

            @pl.when(b == c)
            def _():
                lo, hi = c * TILE, (c + 1) * TILE
                t = t_ref[...]
                if c:
                    w_ref[lo:hi, :lo] = multiply(t, w_ref[lo:hi, :lo], (1, 0))
                w_ref[lo:hi, lo:hi] = t
                if c + 1 < tiles:
                    x = multiply(t, m_ref[lo:hi, hi:], (1, 0))
                    m_ref[hi:, hi:] = m_ref[hi:, hi:] - multiply(x, x, (0, 0))
                    w_ref[hi:, :hi] = w_ref[hi:, :hi] - multiply(x, w_ref[lo:hi, :hi], (0, 0))

        return carry

    lax.fori_loop(0, tiles, body, 0)


def chunk_of(row, number):
    return (row // 2 ^ number // 2) * 2 + (row % 2 ^ number % 2)


def each_chunk(row, refs, use, first=0, last=ROWS):
    for number, ref in enumerate(refs):
        chunk = chunk_of(row, number)

        @pl.when((chunk >= first) & (chunk < last))
        def _():
            use(number, ref, pl.ds(pl.multiple_of((chunk - first) * WIDE, WIDE), WIDE))


def first_kernel(where_ref, own, core, across, both, w_ref, m_ref, t_ref, sems):
    def copy(number, ref, lanes):
        return pltpu.make_async_copy(ref, m_ref.at[:, lanes], sems.at[number])

    row, refs = where_ref[2], (own, core, across, both)
    each_chunk(row, refs, lambda *at: copy(*at).start(), 0, 2)
    each_chunk(row, refs, lambda *at: copy(*at).wait(), 0, 2)
    invert_factor(m_ref, w_ref, t_ref)


def square():
    return pltpu.VMEM((PANEL, PANEL), jnp.float32)


def first_factor(where, pieces):
    return pl.pallas_call(
        first_kernel,
        out_shape=jax.ShapeDtypeStruct((PANEL, PANEL), jnp.float32),
        in_specs=[SMEM] + [HBM] * 4,
        out_specs=VMEM,
        scratch_shapes=[
            square(),
            pltpu.VMEM((TILE, TILE), jnp.float32),
            pltpu.SemaphoreType.DMA((4,)),
        ],
        compiler_params=params(60),
        cost_estimate=pl.CostEstimate(flops=60_000_000_000, bytes_accessed=4 << 20, transcendentals=0),
        name="first_factor",
    )(where, *pieces)


def second_kernel(where_ref, inv_hbm, *refs):
    upper, lower, refs = refs[:4], refs[4:8], refs[8:]
    w_hbm, x_hbm, r_hbm, inv_ref, a_ref, m_ref, w_ref, x_ref, r_ref, t_ref = refs[:10]
    inv_parts, x_parts, sems = refs[10:]

    def copy_upper(number, ref, lanes):
        return pltpu.make_async_copy(ref, a_ref.at[:, lanes], sems.at[number])

    def copy_lower(number, ref, lanes):
        rows = ref.at[pl.ds(0, PANEL), :]
        return pltpu.make_async_copy(rows, m_ref.at[:, lanes], sems.at[4 + number])

    def copy_rows(number, ref, lanes):
        rows = ref.at[pl.ds(PANEL, PANEL), :]
        return pltpu.make_async_copy(rows, r_ref.at[:, lanes], sems.at[8 + number])

    row = where_ref[2]
    inv = pltpu.make_async_copy(inv_hbm, inv_ref, sems.at[12])
    inv.start()
    each_chunk(row, upper, lambda *at: copy_upper(*at).start(), 2, 4)
    each_chunk(row, lower, lambda *at: copy_lower(*at).start(), 2, 4)
    each_chunk(row, lower, lambda *at: copy_rows(*at).start())
    inv.wait()
    inv_parts[0], inv_parts[1] = split(inv_ref[...])
    each_chunk(row, upper, lambda *at: copy_upper(*at).wait(), 2, 4)
    inv = inv_parts[0], inv_parts[1]
    x_ref[...] = contract_split(inv, split(a_ref[...]), (1, 0))
    out = pltpu.make_async_copy(x_ref, x_hbm, sems.at[13])
    out.start()
    x_parts[0], x_parts[1] = split(x_ref[...])
    x = x_parts[0], x_parts[1]
    each_chunk(row, lower, lambda *at: copy_lower(*at).wait(), 2, 4)
    m_ref[...] = m_ref[...] - contract_split(x, x, (0, 0))
    each_chunk(row, lower, lambda *at: copy_rows(*at).wait())

    def rows_out(b):
        rows = pl.ds(pl.multiple_of(b * TILE, TILE), TILE)
        return pltpu.make_async_copy(r_ref.at[rows, :], r_hbm.at[rows, :], sems.at[15 + b])

    def beside(b):
        rows = pl.ds(pl.multiple_of(b * TILE, TILE), TILE)
        first = contract_split(split(r_ref[rows, :PANEL]), (inv_parts[0], inv_parts[1]), (1, 1))
        r_ref[rows, :PANEL] = first
        left = contract_split(split(first), (x_parts[0], x_parts[1]), (1, 0))
        r_ref[rows, PANEL:] = r_ref[rows, PANEL:] - left
        rows_out(b).start()

    invert_factor(m_ref, w_ref, t_ref, beside)
    last = pltpu.make_async_copy(w_ref, w_hbm, sems.at[14])
    last.start()
    for b in range(ROWS):
        rows_out(b).wait()
    out.wait()
    last.wait()


def second_factor(where, inv, upper, lower):
    shape = jax.ShapeDtypeStruct((PANEL, PANEL), jnp.float32)
    return pl.pallas_call(
        second_kernel,
        out_shape=(shape, shape, jax.ShapeDtypeStruct((PANEL, 2 * PANEL), jnp.float32)),
        in_specs=[SMEM] + [HBM] * 9,
        out_specs=(HBM, HBM, HBM),
        scratch_shapes=[
            square(), square(), square(), square(), square(),
            pltpu.VMEM((PANEL, 2 * PANEL), jnp.float32),
            pltpu.VMEM((TILE, TILE), jnp.float32),
            pltpu.VMEM((2, PANEL, PANEL), jnp.bfloat16),
            pltpu.VMEM((2, PANEL, PANEL), jnp.bfloat16),
            pltpu.SemaphoreType.DMA((19,)),
        ],
        compiler_params=params(60),
        cost_estimate=pl.CostEstimate(flops=60_000_000_000, bytes_accessed=8 << 20, transcendentals=0),
        name="second_factor",
    )(where, inv, *upper, *lower)


def finish_kernel(
    where_ref, inv0_hbm, inv1_hbm, x01_hbm, cols_hbm, rows_hbm, front_hbm, out_ref,
    inv0_ref, inv1_ref, x01_ref, rows_ref, cols0_ref, cols1_ref, front_ref, sems,
):
    col, shard = where_ref[1], where_ref[3]
    copies = [
        (inv0_hbm, inv0_ref),
        (cols_hbm.at[:, pl.ds(0, 2 * BLK), :], cols0_ref),
        (cols_hbm.at[:, pl.ds(2 * BLK, 2 * BLK), :], cols1_ref),
        (x01_hbm, x01_ref),
        (inv1_hbm, inv1_ref),
        (rows_hbm, rows_ref),
        (front_hbm, front_ref),
    ]
    copies = [
        pltpu.make_async_copy(source, target, sems.at[i])
        for i, (source, target) in enumerate(copies)
    ]
    for copy in copies:
        copy.start()
    for copy in copies:
        copy.wait()
    inv0, inv1, x01 = split(inv0_ref[...]), split(inv1_ref[...]), split(x01_ref[...])
    r0 = split(rows_ref[:, :PANEL])
    c0 = contract_split(inv0, split(cols0_ref[...].reshape(PANEL, WIDE)), (1, 0))
    cols0_ref[...] = c0.reshape(cols0_ref.shape)
    c0 = split(c0)
    r1 = split(contract_split(split(rows_ref[:, PANEL:]), inv1, (1, 1)))
    c1 = split(cols1_ref[...].reshape(PANEL, WIDE) - contract_split(x01, c0, (0, 0)))
    c1 = contract_split(inv1, c1, (1, 0))
    cols1_ref[...] = c1.reshape(cols1_ref.shape)
    update = contract_split(r0, c0, (1, 0)) + contract_split(r1, split(c1), (1, 0))
    live = (shard >= ROWS).astype(jnp.float32)
    for slot in range(TOP, SHARDS):
        rows = slice(slot * BLK, (slot + 1) * BLK)
        out_ref[slot] = (front_ref[slot] - update[rows]) * live
    past = (shard >= ROWS // 2).astype(jnp.float32)
    for half in range(2):
        rows = slice(half * BLK, (half + 1) * BLK)
        out_ref[half] = cols0_ref[col, rows, :]
        out_ref[2 + half] = cols1_ref[col, rows, :] * past


def finish(where, inv0, inv1, x01, cols, rows, front):
    return pl.pallas_call(
        finish_kernel,
        out_shape=FRONT,
        in_specs=[SMEM] + [HBM] * 6,
        out_specs=VMEM,
        scratch_shapes=[
            square(), square(), square(),
            pltpu.VMEM((PANEL, 2 * PANEL), jnp.float32),
            pltpu.VMEM((COLS, 2 * BLK, WIDE), jnp.float32),
            pltpu.VMEM((COLS, 2 * BLK, WIDE), jnp.float32),
            pltpu.VMEM((SHARDS, BLK, WIDE), jnp.float32),
            pltpu.SemaphoreType.DMA((7,)),
        ],
        compiler_params=params(60),
        name="finish",
    )(where, inv0, inv1, x01, cols, rows, front)


def swap(x, axis, bit):
    return lax.ppermute(x, axis, [(i, i ^ bit) for i in range(ROWS)])


def to_all(x, axis, count):
    return lax.all_to_all(
        jnp.broadcast_to(x[None], (count, *x.shape)), axis, split_axis=0, concat_axis=0, tiled=True
    )


def exchange(x, axis):
    return lax.all_to_all(x, axis, split_axis=0, concat_axis=0, tiled=True)


def over_rows(x):
    across = swap(x, "row", 2)
    return x, swap(x, "row", 1), across, swap(across, "row", 1)


def from_first(x, sub, beside=None):
    for step in (4, 2, 1):
        pairs = [(i, i + step) for i in range(0, SUBS, 2 * step)]
        got = lax.ppermute(x, "sub", pairs)
        if beside is not None and step == 4:
            got, _ = lax.optimization_barrier((got, beside))
        x = jnp.where(sub % (2 * step) == step, got, x)
    return x


def local(parent_front, child_schur, index_map):
    sub, row, col = (lax.axis_index(name) for name in ("sub", "row", "col"))
    shard = sub * ROWS + row
    where = jnp.stack([shard // (SHARDS // 2), col, row, shard]).astype(jnp.int32)
    parent = parent_front.reshape(SHARDS, BLK, WIDE)

    parent_top = from_first(parent[:TOP], sub)
    low = call(
        spread_low_kernel,
        jax.ShapeDtypeStruct((SUBS, 2 * ROWS, BLK, TILE), jnp.float32),
        (where, index_map, child_schur),
        4,
        [pltpu.SMEM((2 * SHARDS * TILE // BLK,), jnp.int32)],
    )
    low = exchange(low.reshape(SHARDS, 2, BLK, TILE), ("sub", "row"))
    tops = call(place_top_kernel, TOPS, (where, index_map, low, parent_top), 6, SOURCES)
    tops, child_late = lax.optimization_barrier((tops, child_schur))
    pivots = exchange(tops, "col")
    spread = call(
        spread_kernel,
        jax.ShapeDtypeStruct((2 * SHARDS, BLK, TILE), jnp.float32),
        (where, index_map, child_late),
        4,
    )
    parent_rest = from_first(parent[TOP:], sub, spread)
    tail = call(
        place_rest_kernel,
        jax.ShapeDtypeStruct((2 * SHARDS, BLK, WIDE), jnp.float32),
        (where, index_map, low, parent_rest, tops, pivots),
        8,
        SOURCES,
    )
    upper = over_rows(pivots[:, :2].reshape(PANEL, WIDE))
    inv0 = first_factor(where, upper)


    spread, _ = lax.optimization_barrier((spread.reshape(SHARDS, 2, BLK, TILE), pivots))
    tail = tail.reshape(2 * PANEL, WIDE)
    received, across, _ = lax.optimization_barrier(
        (exchange(spread, ("sub", "row")), swap(tail, "row", 2), inv0)
    )
    tail = tail, swap(tail, "row", 1), across, swap(across, "row", 1)
    front, tops = call(place_kernel, (FRONT, TOPS), (where, index_map, received, parent), 6, SOURCES)
    inv1, x01, rows = second_factor(where, inv0, upper, tail)
    cols = exchange(tops, "col").reshape(COLS, TOP * BLK, WIDE)
    out = finish(where, inv0, inv1, x01, cols, rows, front)
    return out.reshape(parent_front.shape)


def solution(mesh):
    spec = P(None, "col", None, ("sub", "row"))
    in_specs = (spec, P(("sub", "row", "col"), None), P())
    return jax.shard_map(local, mesh=mesh, in_specs=in_specs, out_specs=spec, check_vma=False)
```

```python
import functools

import jax
import jax.numpy as jnp
from jax import lax
from jax.experimental import pallas as pl
from jax.experimental.pallas import tpu as pltpu
from jax.sharding import PartitionSpec as P

BLK = 16
TILE = 128
STEP = 8
SUBS = 8
ROWS = 4
COLS = 16
SHARDS = SUBS * ROWS
WIDE = 256
PANEL = 512
TOP = 4

VMEM = pl.BlockSpec(memory_space=pltpu.VMEM)
SMEM = pl.BlockSpec(memory_space=pltpu.SMEM)
HBM = pl.BlockSpec(memory_space=pl.ANY)


def params(mib):
    return pltpu.CompilerParams(vmem_limit_bytes=mib << 20)


def split(a):
    high = a.astype(jnp.bfloat16)
    return high, (a - high.astype(jnp.float32)).astype(jnp.bfloat16)


def contract_split(a, b, dims):
    def product(x, y):
        return lax.dot_general(
            x, y, ((dims[:1], dims[1:]), ((), ())), preferred_element_type=jnp.float32
        )

    return product(a[0], b[1]) + product(a[1], b[0]) + product(a[0], b[0])


def spread_kernel(where_ref, map_ref, child_ref, out_ref):
    child = where_ref[0]
    out_ref[...] = jnp.zeros_like(out_ref)
    lane_block = lax.broadcasted_iota(jnp.int32, (BLK, TILE), 1) // BLK

    def body(tile, carry):
        rows = child_ref[:, pl.ds(pl.multiple_of(tile * TILE, TILE), TILE)]
        for part in range(TILE // BLK):
            block = map_ref[child, tile * (TILE // BLK) + part]
            place = block % (TILE // BLK)
            target = block // (TILE // BLK)
            shift = (place - part + TILE // BLK) % (TILE // BLK) * BLK
            moved = pltpu.roll(rows, shift, 1)
            out_ref[target] = jnp.where(lane_block == place, moved, out_ref[target])
        return carry

    lax.fori_loop(0, child_ref.shape[1] // TILE, body, 0)


def spread_low_kernel(where_ref, map_ref, child_hbm, out_ref, from_ref, child_ref, sems):
    copy = pltpu.make_async_copy(child_hbm, child_ref, sems.at[0])
    copy.start()
    child = where_ref[0]
    part = TILE // BLK
    count = 2 * ROWS
    lane_block = lax.broadcasted_iota(jnp.int32, (BLK, TILE), 1) // BLK

    def clear(block, carry):
        from_ref[block] = -1
        return carry

    def note(block, carry):
        from_ref[map_ref[child, block]] = block
        return carry

    lax.fori_loop(0, count * part, clear, 0, unroll=8)
    lax.fori_loop(0, map_ref.shape[1], note, 0, unroll=8)
    copy.wait()
    for target in range(count):
        tile = jnp.zeros((BLK, TILE), jnp.float32)
        for place in range(part):
            block = from_ref[target * part + place]
            source = jnp.maximum(block, 0)
            rows = child_ref[:, pl.ds(pl.multiple_of(source // part * TILE, TILE), TILE)]
            moved = pltpu.roll(rows, (place - source % part + part) % part * BLK, 1)
            tile = jnp.where((lane_block == place) & (block >= 0), moved, tile)
        for sub in range(SUBS):
            out_ref[sub, target] = tile


def find_sources(where_ref, map_ref, from_ref):
    col = where_ref[1]
    for source in range(SHARDS):
        child, number = divmod(source, SHARDS // 2)
        block = map_ref[child, number * COLS + col]
        from_ref[block // (2 * COLS) * 2 + block % 2] = source


def add_block(out_ref, at, parent, received_ref, source):
    for half in range(2):
        lanes = slice(half * TILE, (half + 1) * TILE)
        out_ref[at, :, lanes] = parent[:, lanes] + received_ref[source, half]


def place_kernel(where_ref, map_ref, received_ref, parent_ref, out_ref, top_ref, from_ref):
    find_sources(where_ref, map_ref, from_ref)
    for slot in range(SHARDS):
        add_block(out_ref, slot, parent_ref[slot], received_ref, from_ref[slot])
    for q in range(COLS):
        top_ref[q] = out_ref[:TOP]


def place_top_kernel(where_ref, map_ref, received_ref, parent_ref, top_ref, from_ref):
    find_sources(where_ref, map_ref, from_ref)
    for slot in range(TOP):
        for half in range(2):
            lanes = slice(half * TILE, (half + 1) * TILE)
            block = parent_ref[slot, :, lanes] + received_ref[from_ref[slot], half]
            for q in range(COLS):
                top_ref[q, slot, :, lanes] = block


def place_rest_kernel(
    where_ref, map_ref, received_ref, parent_ref, top_ref, pivots_ref, out_ref, from_ref
):
    find_sources(where_ref, map_ref, from_ref)
    for slot in range(TOP, SHARDS):
        add_block(out_ref, SHARDS + slot, parent_ref[slot - TOP], received_ref, from_ref[slot])
    for q in range(COLS):
        for half in range(2):
            out_ref[2 * q + half] = pivots_ref[q, 2 + half]
    out_ref[SHARDS : SHARDS + TOP] = top_ref[0]


SOURCES = [pltpu.SMEM((SHARDS,), jnp.int32)]
FRONT = jax.ShapeDtypeStruct((SHARDS, BLK, WIDE), jnp.float32)
TOPS = jax.ShapeDtypeStruct((COLS, TOP, BLK, WIDE), jnp.float32)


def call(kernel, out_shape, operands, mib, scratch=(), big=VMEM):
    return pl.pallas_call(
        kernel,
        out_shape=out_shape,
        in_specs=[SMEM, SMEM] + [big] * (len(operands) - 2),
        out_specs=jax.tree.map(lambda _: VMEM, out_shape),
        scratch_shapes=list(scratch),
        compiler_params=params(mib),
        name=kernel.__name__.removesuffix("_kernel"),
    )(*operands)


def tree_sum(terms):
    while len(terms) > 1:
        terms = [sum(terms[i : i + 2]) for i in range(0, len(terms), 2)]
    return terms[0]


def factor_tile(read, out_ref):
    full = (8, TILE)
    groups = TILE // 8
    sub = lax.broadcasted_iota(jnp.int32, full, 0)
    lane = lax.broadcasted_iota(jnp.int32, full, 1)
    a = [read(h) for h in range(groups)]
    e = [jnp.where(lane == sub + 8 * h, jnp.float32(1), jnp.float32(0)) for h in range(groups)]
    for j in range(0, TILE, STEP):
        g, r = divmod(j, 8)
        col = [
            [jnp.broadcast_to(a[h][:, j + t : j + t + 1], full) for t in range(STEP)]
            for h in range(g, groups)
        ]
        p = [
            [jnp.broadcast_to(col[0][t][r + s : r + s + 1, :], full) for t in range(s + 1)]
            for s in range(STEP)
        ]
        ua = [jnp.broadcast_to(a[g][r + s : r + s + 1, :], full) for s in range(STEP)]
        ue = [jnp.broadcast_to(e[g][r + s : r + s + 1, :], full) for s in range(STEP)]
        rd = [None] * STEP
        low = [[None] * STEP for _ in range(STEP)]
        for t in range(STEP):
            rd[t] = 1.0 / p[t][t]
            for s in range(t + 1, STEP):
                low[s][t] = p[s][t] * rd[t]
            for s in range(t + 1, STEP):
                for q in range(t + 1, s + 1):
                    p[s][q] = p[s][q] - low[s][t] * p[q][t]
            for s in range(t + 1, STEP):
                ua[s] = ua[s] - low[s][t] * ua[t]
                ue[s] = ue[s] - low[s][t] * ue[t]
        for s in range(STEP):
            out_ref[j + s : j + s + 1, :] = (ue[s] * lax.rsqrt(p[s][s]))[0:1, :]
        if j + STEP >= TILE:
            break
        za = [ua[s] * rd[s] for s in range(STEP)]
        ze = [ue[s] * rd[s] for s in range(STEP)]
        for t in range(STEP - 1, 0, -1):
            for s in range(t):
                za[s] = za[s] - low[t][s] * za[t]
                ze[s] = ze[s] - low[t][s] * ze[t]
        for h in range(g, groups):
            if h == g and r + STEP >= 8:
                continue
            c = col[h - g]
            da = tree_sum([c[t] * za[t] for t in range(STEP)])
            de = tree_sum([c[t] * ze[t] for t in range(STEP)])
            if h == g:
                da = jnp.where(sub >= r + STEP, da, 0.0)
                de = jnp.where(sub >= r + STEP, de, 0.0)
            a[h] = a[h] - da
            e[h] = e[h] - de


def multiply(a, b, dims):
    return contract_split(split(a), split(b), dims)


def invert_factor(m_ref, w_ref, t_ref, beside=None):
    tiles = m_ref.shape[0] // TILE
    w_ref[...] = jnp.zeros_like(w_ref)

    def body(b, carry):
        low = pl.multiple_of(b * TILE, TILE)
        factor_tile(
            lambda h: m_ref[pl.ds(pl.multiple_of(low + 8 * h, 8), 8), pl.ds(low, TILE)], t_ref
        )
        if beside is not None:
            beside(b)
        for c in range(tiles):

            @pl.when(b == c)
            def _():
                lo, hi = c * TILE, (c + 1) * TILE
                t = t_ref[...]
                if c:
                    w_ref[lo:hi, :lo] = multiply(t, w_ref[lo:hi, :lo], (1, 0))
                w_ref[lo:hi, lo:hi] = t
                if c + 1 < tiles:
                    x = multiply(t, m_ref[lo:hi, hi:], (1, 0))
                    m_ref[hi:, hi:] = m_ref[hi:, hi:] - multiply(x, x, (0, 0))
                    w_ref[hi:, :hi] = w_ref[hi:, :hi] - multiply(x, w_ref[lo:hi, :hi], (0, 0))

        return carry

    lax.fori_loop(0, tiles, body, 0)


def chunk_of(row, number):
    return (row // 2 ^ number // 2) * 2 + (row % 2 ^ number % 2)


def each_chunk(row, refs, use, first=0, last=ROWS):
    for number, ref in enumerate(refs):
        chunk = chunk_of(row, number)

        @pl.when((chunk >= first) & (chunk < last))
        def _():
            use(number, ref, pl.ds(pl.multiple_of((chunk - first) * WIDE, WIDE), WIDE))


def first_kernel(where_ref, own, core, across, both, w_ref, m_ref, t_ref, sems):
    def copy(number, ref, lanes):
        return pltpu.make_async_copy(ref, m_ref.at[:, lanes], sems.at[number])

    row, refs = where_ref[2], (own, core, across, both)
    each_chunk(row, refs, lambda *at: copy(*at).start(), 0, 2)
    each_chunk(row, refs, lambda *at: copy(*at).wait(), 0, 2)
    invert_factor(m_ref, w_ref, t_ref)


def square():
    return pltpu.VMEM((PANEL, PANEL), jnp.float32)


def first_factor(where, pieces):
    return pl.pallas_call(
        first_kernel,
        out_shape=jax.ShapeDtypeStruct((PANEL, PANEL), jnp.float32),
        in_specs=[SMEM] + [HBM] * 4,
        out_specs=VMEM,
        scratch_shapes=[
            square(),
            pltpu.VMEM((TILE, TILE), jnp.float32),
            pltpu.SemaphoreType.DMA((4,)),
        ],
        compiler_params=params(60),
        cost_estimate=pl.CostEstimate(flops=60_000_000_000, bytes_accessed=4 << 20, transcendentals=0),
        name="first_factor",
    )(where, *pieces)


def second_kernel(where_ref, inv_hbm, *refs):
    upper, lower, refs = refs[:4], refs[4:8], refs[8:]
    w_hbm, x_hbm, r_hbm, inv_ref, a_ref, m_ref, w_ref, x_ref, r_ref, t_ref = refs[:10]
    inv_parts, x_parts, sems = refs[10:]

    def copy_upper(number, ref, lanes):
        return pltpu.make_async_copy(ref, a_ref.at[:, lanes], sems.at[number])

    def copy_lower(number, ref, lanes):
        rows = ref.at[pl.ds(0, PANEL), :]
        return pltpu.make_async_copy(rows, m_ref.at[:, lanes], sems.at[4 + number])

    def copy_rows(number, ref, lanes):
        rows = ref.at[pl.ds(PANEL, PANEL), :]
        return pltpu.make_async_copy(rows, r_ref.at[:, lanes], sems.at[8 + number])

    row = where_ref[2]
    inv = pltpu.make_async_copy(inv_hbm, inv_ref, sems.at[12])
    inv.start()
    each_chunk(row, upper, lambda *at: copy_upper(*at).start(), 2, 4)
    each_chunk(row, lower, lambda *at: copy_lower(*at).start(), 2, 4)
    each_chunk(row, lower, lambda *at: copy_rows(*at).start())
    inv.wait()
    inv_parts[0], inv_parts[1] = split(inv_ref[...])
    each_chunk(row, upper, lambda *at: copy_upper(*at).wait(), 2, 4)
    inv = inv_parts[0], inv_parts[1]
    x_ref[...] = contract_split(inv, split(a_ref[...]), (1, 0))
    out = pltpu.make_async_copy(x_ref, x_hbm, sems.at[13])
    out.start()
    x_parts[0], x_parts[1] = split(x_ref[...])
    x = x_parts[0], x_parts[1]
    each_chunk(row, lower, lambda *at: copy_lower(*at).wait(), 2, 4)
    m_ref[...] = m_ref[...] - contract_split(x, x, (0, 0))
    each_chunk(row, lower, lambda *at: copy_rows(*at).wait())

    def rows_out(b):
        rows = pl.ds(pl.multiple_of(b * TILE, TILE), TILE)
        return pltpu.make_async_copy(r_ref.at[rows, :], r_hbm.at[rows, :], sems.at[15 + b])

    def beside(b):
        rows = pl.ds(pl.multiple_of(b * TILE, TILE), TILE)
        first = contract_split(split(r_ref[rows, :PANEL]), (inv_parts[0], inv_parts[1]), (1, 1))
        r_ref[rows, :PANEL] = first
        left = contract_split(split(first), (x_parts[0], x_parts[1]), (1, 0))
        r_ref[rows, PANEL:] = r_ref[rows, PANEL:] - left
        rows_out(b).start()

    invert_factor(m_ref, w_ref, t_ref, beside)
    last = pltpu.make_async_copy(w_ref, w_hbm, sems.at[14])
    last.start()
    for b in range(ROWS):
        rows_out(b).wait()
    out.wait()
    last.wait()


def second_factor(where, inv, upper, lower):
    shape = jax.ShapeDtypeStruct((PANEL, PANEL), jnp.float32)
    return pl.pallas_call(
        second_kernel,
        out_shape=(shape, shape, jax.ShapeDtypeStruct((PANEL, 2 * PANEL), jnp.float32)),
        in_specs=[SMEM] + [HBM] * 9,
        out_specs=(HBM, HBM, HBM),
        scratch_shapes=[
            square(), square(), square(), square(), square(),
            pltpu.VMEM((PANEL, 2 * PANEL), jnp.float32),
            pltpu.VMEM((TILE, TILE), jnp.float32),
            pltpu.VMEM((2, PANEL, PANEL), jnp.bfloat16),
            pltpu.VMEM((2, PANEL, PANEL), jnp.bfloat16),
            pltpu.SemaphoreType.DMA((19,)),
        ],
        compiler_params=params(60),
        cost_estimate=pl.CostEstimate(flops=60_000_000_000, bytes_accessed=8 << 20, transcendentals=0),
        name="second_factor",
    )(where, inv, *upper, *lower)


def finish_kernel(
    where_ref, inv0_hbm, inv1_hbm, x01_hbm, cols_hbm, rows_hbm, front_hbm, out_ref,
    inv0_ref, inv1_ref, x01_ref, rows_ref, cols0_ref, cols1_ref, front_ref, sems,
):
    col, shard = where_ref[1], where_ref[3]
    copies = [
        (inv0_hbm, inv0_ref),
        (cols_hbm.at[:, pl.ds(0, 2 * BLK), :], cols0_ref),
        (cols_hbm.at[:, pl.ds(2 * BLK, 2 * BLK), :], cols1_ref),
        (x01_hbm, x01_ref),
        (inv1_hbm, inv1_ref),
        (rows_hbm, rows_ref),
        (front_hbm, front_ref),
    ]
    copies = [
        pltpu.make_async_copy(source, target, sems.at[i])
        for i, (source, target) in enumerate(copies)
    ]
    for copy in copies:
        copy.start()
    for copy in copies:
        copy.wait()
    inv0, inv1, x01 = split(inv0_ref[...]), split(inv1_ref[...]), split(x01_ref[...])
    r0 = split(rows_ref[:, :PANEL])
    c0 = contract_split(inv0, split(cols0_ref[...].reshape(PANEL, WIDE)), (1, 0))
    cols0_ref[...] = c0.reshape(cols0_ref.shape)
    c0 = split(c0)
    r1 = split(contract_split(split(rows_ref[:, PANEL:]), inv1, (1, 1)))
    c1 = split(cols1_ref[...].reshape(PANEL, WIDE) - contract_split(x01, c0, (0, 0)))
    c1 = contract_split(inv1, c1, (1, 0))
    cols1_ref[...] = c1.reshape(cols1_ref.shape)
    update = contract_split(r0, c0, (1, 0)) + contract_split(r1, split(c1), (1, 0))
    live = (shard >= ROWS).astype(jnp.float32)
    for slot in range(TOP, SHARDS):
        rows = slice(slot * BLK, (slot + 1) * BLK)
        out_ref[slot] = (front_ref[slot] - update[rows]) * live
    past = (shard >= ROWS // 2).astype(jnp.float32)
    for half in range(2):
        rows = slice(half * BLK, (half + 1) * BLK)
        out_ref[half] = cols0_ref[col, rows, :]
        out_ref[2 + half] = cols1_ref[col, rows, :] * past


def finish(where, inv0, inv1, x01, cols, rows, front):
    return pl.pallas_call(
        finish_kernel,
        out_shape=FRONT,
        in_specs=[SMEM] + [HBM] * 6,
        out_specs=VMEM,
        scratch_shapes=[
            square(), square(), square(),
            pltpu.VMEM((PANEL, 2 * PANEL), jnp.float32),
            pltpu.VMEM((COLS, 2 * BLK, WIDE), jnp.float32),
            pltpu.VMEM((COLS, 2 * BLK, WIDE), jnp.float32),
            pltpu.VMEM((SHARDS, BLK, WIDE), jnp.float32),
            pltpu.SemaphoreType.DMA((7,)),
        ],
        compiler_params=params(60),
        name="finish",
    )(where, inv0, inv1, x01, cols, rows, front)


def swap(x, axis, bit):
    return lax.ppermute(x, axis, [(i, i ^ bit) for i in range(ROWS)])


def to_all(x, axis, count):
    return lax.all_to_all(
        jnp.broadcast_to(x[None], (count, *x.shape)), axis, split_axis=0, concat_axis=0, tiled=True
    )


def exchange(x, axis):
    return lax.all_to_all(x, axis, split_axis=0, concat_axis=0, tiled=True)


def over_rows(x):
    across = swap(x, "row", 2)
    return x, swap(x, "row", 1), across, swap(across, "row", 1)


def from_first(x, sub, beside=None):
    for step in (4, 2, 1):
        pairs = [(i, i + step) for i in range(0, SUBS, 2 * step)]
        got = lax.ppermute(x, "sub", pairs)
        if beside is not None and step == 4:
            got, _ = lax.optimization_barrier((got, beside))
        x = jnp.where(sub % (2 * step) == step, got, x)
    return x


def local(parent_front, child_schur, index_map):
    sub, row, col = (lax.axis_index(name) for name in ("sub", "row", "col"))
    shard = sub * ROWS + row
    where = jnp.stack([shard // (SHARDS // 2), col, row, shard]).astype(jnp.int32)
    parent = parent_front.reshape(SHARDS, BLK, WIDE)

    parent_top = from_first(parent[:TOP], sub)
    low = call(
        spread_low_kernel,
        jax.ShapeDtypeStruct((SUBS, 2 * ROWS, BLK, TILE), jnp.float32),
        (where, index_map, child_schur),
        60,
        [
            pltpu.SMEM((2 * SHARDS * TILE // BLK,), jnp.int32),
            pltpu.VMEM(child_schur.shape, child_schur.dtype),
            pltpu.SemaphoreType.DMA((1,)),
        ],
        big=HBM,
    )
    low = exchange(low.reshape(SHARDS, 2, BLK, TILE), ("sub", "row"))
    tops = call(place_top_kernel, TOPS, (where, index_map, low, parent_top), 6, SOURCES)
    tops, child_late = lax.optimization_barrier((tops, child_schur))
    pivots = exchange(tops, "col")
    spread = call(
        spread_kernel,
        jax.ShapeDtypeStruct((2 * SHARDS, BLK, TILE), jnp.float32),
        (where, index_map, child_late),
        4,
    )
    parent_rest = from_first(parent[TOP:], sub, spread)
    tail = call(
        place_rest_kernel,
        jax.ShapeDtypeStruct((2 * SHARDS, BLK, WIDE), jnp.float32),
        (where, index_map, low, parent_rest, tops, pivots),
        8,
        SOURCES,
    )
    upper = over_rows(pivots[:, :2].reshape(PANEL, WIDE))
    inv0 = first_factor(where, upper)


    spread, _ = lax.optimization_barrier((spread.reshape(SHARDS, 2, BLK, TILE), pivots))
    tail = tail.reshape(2 * PANEL, WIDE)
    received, across, _ = lax.optimization_barrier(
        (exchange(spread, ("sub", "row")), swap(tail, "row", 2), inv0)
    )
    tail = tail, swap(tail, "row", 1), across, swap(across, "row", 1)
    front, tops = call(place_kernel, (FRONT, TOPS), (where, index_map, received, parent), 6, SOURCES)
    inv1, x01, rows = second_factor(where, inv0, upper, tail)
    cols = exchange(tops, "col").reshape(COLS, TOP * BLK, WIDE)
    out = finish(where, inv0, inv1, x01, cols, rows, front)
    return out.reshape(parent_front.shape)


def solution(mesh):
    spec = P(None, "col", None, ("sub", "row"))
    in_specs = (spec, P(("sub", "row", "col"), None), P())
    return jax.shard_map(local, mesh=mesh, in_specs=in_specs, out_specs=spec, check_vma=False)
```

```python
import functools

import jax
import jax.numpy as jnp
from jax import lax
from jax.experimental import pallas as pl
from jax.experimental.pallas import tpu as pltpu
from jax.sharding import PartitionSpec as P

BLK = 16
TILE = 128
STEP = 8
SUBS = 8
ROWS = 4
COLS = 16
SHARDS = SUBS * ROWS
WIDE = 256
PANEL = 512
TOP = 4

VMEM = pl.BlockSpec(memory_space=pltpu.VMEM)
SMEM = pl.BlockSpec(memory_space=pltpu.SMEM)
HBM = pl.BlockSpec(memory_space=pl.ANY)


def params(mib):
    return pltpu.CompilerParams(vmem_limit_bytes=mib << 20)


def split(a):
    high = a.astype(jnp.bfloat16)
    return high, (a - high.astype(jnp.float32)).astype(jnp.bfloat16)


def contract_split(a, b, dims):
    def product(x, y):
        return lax.dot_general(
            x, y, ((dims[:1], dims[1:]), ((), ())), preferred_element_type=jnp.float32
        )

    return product(a[0], b[1]) + product(a[1], b[0]) + product(a[0], b[0])


def cut(parts, rows, lanes):
    return parts[0][rows, lanes], parts[1][rows, lanes]


def inverse_times(inv, b):
    near, far, every = slice(0, WIDE), slice(WIDE, PANEL), slice(None)
    top = contract_split(cut(inv, near, near), cut(b, near, every), (1, 0))
    return jnp.concatenate([top, contract_split(cut(inv, far, every), b, (1, 0))], axis=0)


def times_inverse_t(a, inv):
    near, far, every = slice(0, WIDE), slice(WIDE, PANEL), slice(None)
    left = contract_split(cut(a, every, near), cut(inv, near, near), (1, 1))
    return jnp.concatenate([left, contract_split(a, cut(inv, far, every), (1, 1))], axis=1)


def spread_kernel(where_ref, map_ref, child_ref, out_ref):
    child = where_ref[0]
    out_ref[...] = jnp.zeros_like(out_ref)
    lane_block = lax.broadcasted_iota(jnp.int32, (BLK, TILE), 1) // BLK

    def body(tile, carry):
        rows = child_ref[:, pl.ds(pl.multiple_of(tile * TILE, TILE), TILE)]
        for part in range(TILE // BLK):
            block = map_ref[child, tile * (TILE // BLK) + part]
            place = block % (TILE // BLK)
            target = block // (TILE // BLK)
            shift = (place - part + TILE // BLK) % (TILE // BLK) * BLK
            moved = pltpu.roll(rows, shift, 1)
            out_ref[target] = jnp.where(lane_block == place, moved, out_ref[target])
        return carry

    lax.fori_loop(0, child_ref.shape[1] // TILE, body, 0)


def spread_low_kernel(where_ref, map_ref, child_hbm, out_ref, from_ref, child_ref, sems):
    copy = pltpu.make_async_copy(child_hbm, child_ref, sems.at[0])
    copy.start()
    child = where_ref[0]
    part = TILE // BLK
    count = 2 * ROWS
    lane_block = lax.broadcasted_iota(jnp.int32, (BLK, TILE), 1) // BLK

    def clear(block, carry):
        from_ref[block] = -1
        return carry

    def note(block, carry):
        from_ref[map_ref[child, block]] = block
        return carry

    lax.fori_loop(0, count * part, clear, 0, unroll=8)
    lax.fori_loop(0, map_ref.shape[1], note, 0, unroll=8)
    copy.wait()
    for target in range(count):
        tile = jnp.zeros((BLK, TILE), jnp.float32)
        for place in range(part):
            block = from_ref[target * part + place]
            source = jnp.maximum(block, 0)
            rows = child_ref[:, pl.ds(pl.multiple_of(source // part * TILE, TILE), TILE)]
            moved = pltpu.roll(rows, (place - source % part + part) % part * BLK, 1)
            tile = jnp.where((lane_block == place) & (block >= 0), moved, tile)
        for sub in range(SUBS):
            out_ref[sub, target] = tile


def find_sources(where_ref, map_ref, from_ref):
    col = where_ref[1]
    for source in range(SHARDS):
        child, number = divmod(source, SHARDS // 2)
        block = map_ref[child, number * COLS + col]
        from_ref[block // (2 * COLS) * 2 + block % 2] = source


def add_block(out_ref, at, parent, received_ref, source):
    for half in range(2):
        lanes = slice(half * TILE, (half + 1) * TILE)
        out_ref[at, :, lanes] = parent[:, lanes] + received_ref[source, half]


def place_kernel(where_ref, map_ref, received_ref, parent_ref, out_ref, top_ref, from_ref):
    find_sources(where_ref, map_ref, from_ref)
    for slot in range(SHARDS):
        add_block(out_ref, slot, parent_ref[slot], received_ref, from_ref[slot])
    for q in range(COLS):
        top_ref[q] = out_ref[:TOP]


def place_top_kernel(where_ref, map_ref, received_ref, parent_ref, top_ref, from_ref):
    find_sources(where_ref, map_ref, from_ref)
    for slot in range(TOP):
        for half in range(2):
            lanes = slice(half * TILE, (half + 1) * TILE)
            block = parent_ref[slot, :, lanes] + received_ref[from_ref[slot], half]
            for q in range(COLS):
                top_ref[q, slot, :, lanes] = block


def place_rest_kernel(
    where_ref, map_ref, received_ref, parent_ref, top_ref, pivots_ref, out_ref, from_ref
):
    find_sources(where_ref, map_ref, from_ref)
    for slot in range(TOP, SHARDS):
        add_block(out_ref, SHARDS + slot, parent_ref[slot - TOP], received_ref, from_ref[slot])
    for q in range(COLS):
        for half in range(2):
            out_ref[2 * q + half] = pivots_ref[q, 2 + half]
    out_ref[SHARDS : SHARDS + TOP] = top_ref[0]


SOURCES = [pltpu.SMEM((SHARDS,), jnp.int32)]
FRONT = jax.ShapeDtypeStruct((SHARDS, BLK, WIDE), jnp.float32)
TOPS = jax.ShapeDtypeStruct((COLS, TOP, BLK, WIDE), jnp.float32)


def call(kernel, out_shape, operands, mib, scratch=(), big=VMEM):
    return pl.pallas_call(
        kernel,
        out_shape=out_shape,
        in_specs=[SMEM, SMEM] + [big] * (len(operands) - 2),
        out_specs=jax.tree.map(lambda _: VMEM, out_shape),
        scratch_shapes=list(scratch),
        compiler_params=params(mib),
        name=kernel.__name__.removesuffix("_kernel"),
    )(*operands)


def tree_sum(terms):
    while len(terms) > 1:
        terms = [sum(terms[i : i + 2]) for i in range(0, len(terms), 2)]
    return terms[0]


def factor_tile(read, out_ref):
    full = (8, TILE)
    groups = TILE // 8
    sub = lax.broadcasted_iota(jnp.int32, full, 0)
    lane = lax.broadcasted_iota(jnp.int32, full, 1)
    a = [read(h) for h in range(groups)]
    e = [jnp.where(lane == sub + 8 * h, jnp.float32(1), jnp.float32(0)) for h in range(groups)]
    for j in range(0, TILE, STEP):
        g, r = divmod(j, 8)
        col = [
            [jnp.broadcast_to(a[h][:, j + t : j + t + 1], full) for t in range(STEP)]
            for h in range(g, groups)
        ]
        p = [
            [jnp.broadcast_to(col[0][t][r + s : r + s + 1, :], full) for t in range(s + 1)]
            for s in range(STEP)
        ]
        ua = [jnp.broadcast_to(a[g][r + s : r + s + 1, :], full) for s in range(STEP)]
        ue = [jnp.broadcast_to(e[g][r + s : r + s + 1, :], full) for s in range(STEP)]
        rd = [None] * STEP
        low = [[None] * STEP for _ in range(STEP)]
        for t in range(STEP):
            rd[t] = 1.0 / p[t][t]
            for s in range(t + 1, STEP):
                low[s][t] = p[s][t] * rd[t]
            for s in range(t + 1, STEP):
                for q in range(t + 1, s + 1):
                    p[s][q] = p[s][q] - low[s][t] * p[q][t]
            for s in range(t + 1, STEP):
                ua[s] = ua[s] - low[s][t] * ua[t]
                ue[s] = ue[s] - low[s][t] * ue[t]
        for s in range(STEP):
            out_ref[j + s : j + s + 1, :] = (ue[s] * lax.rsqrt(p[s][s]))[0:1, :]
        if j + STEP >= TILE:
            break
        za = [ua[s] * rd[s] for s in range(STEP)]
        ze = [ue[s] * rd[s] for s in range(STEP)]
        for t in range(STEP - 1, 0, -1):
            for s in range(t):
                za[s] = za[s] - low[t][s] * za[t]
                ze[s] = ze[s] - low[t][s] * ze[t]
        for h in range(g, groups):
            if h == g and r + STEP >= 8:
                continue
            c = col[h - g]
            da = tree_sum([c[t] * za[t] for t in range(STEP)])
            de = tree_sum([c[t] * ze[t] for t in range(STEP)])
            if h == g:
                da = jnp.where(sub >= r + STEP, da, 0.0)
                de = jnp.where(sub >= r + STEP, de, 0.0)
            a[h] = a[h] - da
            e[h] = e[h] - de


def multiply(a, b, dims):
    return contract_split(split(a), split(b), dims)


def invert_factor(m_ref, w_ref, t_ref, beside=None):
    tiles = m_ref.shape[0] // TILE
    w_ref[...] = jnp.zeros_like(w_ref)

    def body(b, carry):
        low = pl.multiple_of(b * TILE, TILE)
        factor_tile(
            lambda h: m_ref[pl.ds(pl.multiple_of(low + 8 * h, 8), 8), pl.ds(low, TILE)], t_ref
        )
        if beside is not None:
            beside(b)
        for c in range(tiles):

            @pl.when(b == c)
            def _():
                lo, hi = c * TILE, (c + 1) * TILE
                t = t_ref[...]
                if c:
                    w_ref[lo:hi, :lo] = multiply(t, w_ref[lo:hi, :lo], (1, 0))
                w_ref[lo:hi, lo:hi] = t
                if c + 1 < tiles:
                    x = multiply(t, m_ref[lo:hi, hi:], (1, 0))
                    m_ref[hi:, hi:] = m_ref[hi:, hi:] - multiply(x, x, (0, 0))
                    w_ref[hi:, :hi] = w_ref[hi:, :hi] - multiply(x, w_ref[lo:hi, :hi], (0, 0))

        return carry

    lax.fori_loop(0, tiles, body, 0)


def chunk_of(row, number):
    return (row // 2 ^ number // 2) * 2 + (row % 2 ^ number % 2)


def each_chunk(row, refs, use, first=0, last=ROWS):
    for number, ref in enumerate(refs):
        chunk = chunk_of(row, number)

        @pl.when((chunk >= first) & (chunk < last))
        def _():
            use(number, ref, pl.ds(pl.multiple_of((chunk - first) * WIDE, WIDE), WIDE))


def first_kernel(where_ref, own, core, across, both, w_ref, m_ref, t_ref, sems):
    def copy(number, ref, lanes):
        return pltpu.make_async_copy(ref, m_ref.at[:, lanes], sems.at[number])

    row, refs = where_ref[2], (own, core, across, both)
    each_chunk(row, refs, lambda *at: copy(*at).start(), 0, 2)
    each_chunk(row, refs, lambda *at: copy(*at).wait(), 0, 2)
    invert_factor(m_ref, w_ref, t_ref)


def square():
    return pltpu.VMEM((PANEL, PANEL), jnp.float32)


def first_factor(where, pieces):
    return pl.pallas_call(
        first_kernel,
        out_shape=jax.ShapeDtypeStruct((PANEL, PANEL), jnp.float32),
        in_specs=[SMEM] + [HBM] * 4,
        out_specs=VMEM,
        scratch_shapes=[
            square(),
            pltpu.VMEM((TILE, TILE), jnp.float32),
            pltpu.SemaphoreType.DMA((4,)),
        ],
        compiler_params=params(60),
        cost_estimate=pl.CostEstimate(flops=60_000_000_000, bytes_accessed=4 << 20, transcendentals=0),
        name="first_factor",
    )(where, *pieces)


def second_kernel(where_ref, inv_hbm, *refs):
    upper, lower, refs = refs[:4], refs[4:8], refs[8:]
    w_hbm, x_hbm, r_hbm, inv_ref, a_ref, m_ref, w_ref, x_ref, r_ref, t_ref = refs[:10]
    inv_parts, x_parts, sems = refs[10:]

    def copy_upper(number, ref, lanes):
        return pltpu.make_async_copy(ref, a_ref.at[:, lanes], sems.at[number])

    def copy_lower(number, ref, lanes):
        rows = ref.at[pl.ds(0, PANEL), :]
        return pltpu.make_async_copy(rows, m_ref.at[:, lanes], sems.at[4 + number])

    def copy_rows(number, ref, lanes):
        rows = ref.at[pl.ds(PANEL, PANEL), :]
        return pltpu.make_async_copy(rows, r_ref.at[:, lanes], sems.at[8 + number])

    row = where_ref[2]
    inv = pltpu.make_async_copy(inv_hbm, inv_ref, sems.at[12])
    inv.start()
    each_chunk(row, upper, lambda *at: copy_upper(*at).start(), 2, 4)
    each_chunk(row, lower, lambda *at: copy_lower(*at).start(), 2, 4)
    each_chunk(row, lower, lambda *at: copy_rows(*at).start())
    inv.wait()
    inv_parts[0], inv_parts[1] = split(inv_ref[...])
    each_chunk(row, upper, lambda *at: copy_upper(*at).wait(), 2, 4)
    inv = inv_parts[0], inv_parts[1]
    x_ref[...] = contract_split(inv, split(a_ref[...]), (1, 0))
    out = pltpu.make_async_copy(x_ref, x_hbm, sems.at[13])
    out.start()
    x_parts[0], x_parts[1] = split(x_ref[...])
    x = x_parts[0], x_parts[1]
    each_chunk(row, lower, lambda *at: copy_lower(*at).wait(), 2, 4)
    m_ref[...] = m_ref[...] - contract_split(x, x, (0, 0))
    each_chunk(row, lower, lambda *at: copy_rows(*at).wait())

    def rows_out(b):
        rows = pl.ds(pl.multiple_of(b * TILE, TILE), TILE)
        return pltpu.make_async_copy(r_ref.at[rows, :], r_hbm.at[rows, :], sems.at[15 + b])

    def beside(b):
        rows = pl.ds(pl.multiple_of(b * TILE, TILE), TILE)
        first = contract_split(split(r_ref[rows, :PANEL]), (inv_parts[0], inv_parts[1]), (1, 1))
        r_ref[rows, :PANEL] = first
        left = contract_split(split(first), (x_parts[0], x_parts[1]), (1, 0))
        r_ref[rows, PANEL:] = r_ref[rows, PANEL:] - left
        rows_out(b).start()

    invert_factor(m_ref, w_ref, t_ref, beside)
    last = pltpu.make_async_copy(w_ref, w_hbm, sems.at[14])
    last.start()
    for b in range(ROWS):
        rows_out(b).wait()
    out.wait()
    last.wait()


def second_factor(where, inv, upper, lower):
    shape = jax.ShapeDtypeStruct((PANEL, PANEL), jnp.float32)
    return pl.pallas_call(
        second_kernel,
        out_shape=(shape, shape, jax.ShapeDtypeStruct((PANEL, 2 * PANEL), jnp.float32)),
        in_specs=[SMEM] + [HBM] * 9,
        out_specs=(HBM, HBM, HBM),
        scratch_shapes=[
            square(), square(), square(), square(), square(),
            pltpu.VMEM((PANEL, 2 * PANEL), jnp.float32),
            pltpu.VMEM((TILE, TILE), jnp.float32),
            pltpu.VMEM((2, PANEL, PANEL), jnp.bfloat16),
            pltpu.VMEM((2, PANEL, PANEL), jnp.bfloat16),
            pltpu.SemaphoreType.DMA((19,)),
        ],
        compiler_params=params(60),
        cost_estimate=pl.CostEstimate(flops=60_000_000_000, bytes_accessed=8 << 20, transcendentals=0),
        name="second_factor",
    )(where, inv, *upper, *lower)


def finish_kernel(
    where_ref, inv0_hbm, inv1_hbm, x01_hbm, cols_hbm, rows_hbm, front_hbm, out_ref,
    inv0_ref, inv1_ref, x01_ref, rows_ref, cols0_ref, cols1_ref, front_ref, sems,
):
    col, shard = where_ref[1], where_ref[3]
    copies = [
        (inv0_hbm, inv0_ref),
        (cols_hbm.at[:, pl.ds(0, 2 * BLK), :], cols0_ref),
        (cols_hbm.at[:, pl.ds(2 * BLK, 2 * BLK), :], cols1_ref),
        (x01_hbm, x01_ref),
        (inv1_hbm, inv1_ref),
        (rows_hbm, rows_ref),
        (front_hbm, front_ref),
    ]
    copies = [
        pltpu.make_async_copy(source, target, sems.at[i])
        for i, (source, target) in enumerate(copies)
    ]
    for copy in copies:
        copy.start()
    for copy in copies:
        copy.wait()
    inv0, inv1, x01 = split(inv0_ref[...]), split(inv1_ref[...]), split(x01_ref[...])
    r0 = split(rows_ref[:, :PANEL])
    c0 = inverse_times(inv0, split(cols0_ref[...].reshape(PANEL, WIDE)))
    cols0_ref[...] = c0.reshape(cols0_ref.shape)
    c0 = split(c0)
    r1 = split(times_inverse_t(split(rows_ref[:, PANEL:]), inv1))
    c1 = split(cols1_ref[...].reshape(PANEL, WIDE) - contract_split(x01, c0, (0, 0)))
    c1 = inverse_times(inv1, c1)
    cols1_ref[...] = c1.reshape(cols1_ref.shape)
    update = contract_split(r0, c0, (1, 0)) + contract_split(r1, split(c1), (1, 0))
    live = (shard >= ROWS).astype(jnp.float32)
    for slot in range(TOP, SHARDS):
        rows = slice(slot * BLK, (slot + 1) * BLK)
        out_ref[slot] = (front_ref[slot] - update[rows]) * live
    past = (shard >= ROWS // 2).astype(jnp.float32)
    for half in range(2):
        rows = slice(half * BLK, (half + 1) * BLK)
        out_ref[half] = cols0_ref[col, rows, :]
        out_ref[2 + half] = cols1_ref[col, rows, :] * past


def finish(where, inv0, inv1, x01, cols, rows, front):
    return pl.pallas_call(
        finish_kernel,
        out_shape=FRONT,
        in_specs=[SMEM] + [HBM] * 6,
        out_specs=VMEM,
        scratch_shapes=[
            square(), square(), square(),
            pltpu.VMEM((PANEL, 2 * PANEL), jnp.float32),
            pltpu.VMEM((COLS, 2 * BLK, WIDE), jnp.float32),
            pltpu.VMEM((COLS, 2 * BLK, WIDE), jnp.float32),
            pltpu.VMEM((SHARDS, BLK, WIDE), jnp.float32),
            pltpu.SemaphoreType.DMA((7,)),
        ],
        compiler_params=params(60),
        name="finish",
    )(where, inv0, inv1, x01, cols, rows, front)


def swap(x, axis, bit):
    return lax.ppermute(x, axis, [(i, i ^ bit) for i in range(ROWS)])


def to_all(x, axis, count):
    return lax.all_to_all(
        jnp.broadcast_to(x[None], (count, *x.shape)), axis, split_axis=0, concat_axis=0, tiled=True
    )


def exchange(x, axis):
    return lax.all_to_all(x, axis, split_axis=0, concat_axis=0, tiled=True)


def over_rows(x):
    across = swap(x, "row", 2)
    return x, swap(x, "row", 1), across, swap(across, "row", 1)


def from_first(x, sub, beside=None):
    for step in (4, 2, 1):
        pairs = [(i, i + step) for i in range(0, SUBS, 2 * step)]
        got = lax.ppermute(x, "sub", pairs)
        if beside is not None and step == 4:
            got, _ = lax.optimization_barrier((got, beside))
        x = jnp.where(sub % (2 * step) == step, got, x)
    return x


def local(parent_front, child_schur, index_map):
    sub, row, col = (lax.axis_index(name) for name in ("sub", "row", "col"))
    shard = sub * ROWS + row
    where = jnp.stack([shard // (SHARDS // 2), col, row, shard]).astype(jnp.int32)
    parent = parent_front.reshape(SHARDS, BLK, WIDE)

    parent_top = from_first(parent[:TOP], sub)
    low = call(
        spread_low_kernel,
        jax.ShapeDtypeStruct((SUBS, 2 * ROWS, BLK, TILE), jnp.float32),
        (where, index_map, child_schur),
        60,
        [
            pltpu.SMEM((2 * SHARDS * TILE // BLK,), jnp.int32),
            pltpu.VMEM(child_schur.shape, child_schur.dtype),
            pltpu.SemaphoreType.DMA((1,)),
        ],
        big=HBM,
    )
    low = exchange(low.reshape(SHARDS, 2, BLK, TILE), ("sub", "row"))
    tops = call(place_top_kernel, TOPS, (where, index_map, low, parent_top), 6, SOURCES)
    tops, child_late = lax.optimization_barrier((tops, child_schur))
    pivots = exchange(tops, "col")
    spread = call(
        spread_kernel,
        jax.ShapeDtypeStruct((2 * SHARDS, BLK, TILE), jnp.float32),
        (where, index_map, child_late),
        4,
    )
    parent_rest = from_first(parent[TOP:], sub, spread)
    tail = call(
        place_rest_kernel,
        jax.ShapeDtypeStruct((2 * SHARDS, BLK, WIDE), jnp.float32),
        (where, index_map, low, parent_rest, tops, pivots),
        8,
        SOURCES,
    )
    upper = over_rows(pivots[:, :2].reshape(PANEL, WIDE))
    inv0 = first_factor(where, upper)


    spread, _ = lax.optimization_barrier((spread.reshape(SHARDS, 2, BLK, TILE), pivots))
    tail = tail.reshape(2 * PANEL, WIDE)
    received, across, _ = lax.optimization_barrier(
        (exchange(spread, ("sub", "row")), swap(tail, "row", 2), inv0)
    )
    tail = tail, swap(tail, "row", 1), across, swap(across, "row", 1)
    front, tops = call(place_kernel, (FRONT, TOPS), (where, index_map, received, parent), 6, SOURCES)
    inv1, x01, rows = second_factor(where, inv0, upper, tail)
    cols = exchange(tops, "col").reshape(COLS, TOP * BLK, WIDE)
    out = finish(where, inv0, inv1, x01, cols, rows, front)
    return out.reshape(parent_front.shape)


def solution(mesh):
    spec = P(None, "col", None, ("sub", "row"))
    in_specs = (spec, P(("sub", "row", "col"), None), P())
    return jax.shard_map(local, mesh=mesh, in_specs=in_specs, out_specs=spec, check_vma=False)
```
